128 devices in a mesh: grp: 2 (over core), shard: 64 (over z, y, x).
Axes of the slice: x: 4, y: 4, z: 4, core: 2. Of those that a mesh axis runs over, the one named last changes fastest.
Arguments:
- tokens: bfloat16 [32768, 1536], P(('grp', 'shard')), may hold values from -6 to 6
- segment_ids: int32 [128, 256], P(('grp', 'shard')), may hold values from 0 to 7, never falling along the last dimension, each value on 1 to 128 neighbouring positions
- norm_gain: float32 [1536], replicated, may hold values from 0.5 to 1.5
- in_weight: bfloat16 [1536, 6448], P('shard'), may hold values from -0.15625 to 0.15625
- conv_weight: float32 [4, 3328], replicated, may hold values from -3 to 3
- conv_bias: float32 [3328], replicated, may hold values from -2 to 2
- dt_bias: float32 [48], replicated, may hold values from -5 to -2
- a_log: float32 [48], replicated, may hold values from -0.5 to 2.5
- skip_d: float32 [48], replicated, may hold values from 0.5 to 1.5
- gnorm_gain: float32 [3072], replicated, may hold values from 0.5 to 1.5
- out_weight: bfloat16 [3072, 1536], P('shard'), may hold values from -0.109375 to 0.109375
- cotangent: bfloat16 [32768, 1536], P(('grp', 'shard')), may hold values from -6 to 6
Outputs:
- out_tokens: bfloat16 [32768, 1536], P(('grp', 'shard'))
- grad_tokens: float32 [32768, 1536], P(('grp', 'shard'))
- grad_norm_gain: float32 [1536], replicated
- grad_in_weight: float32 [1536, 6448], P('shard')
- grad_conv_weight: float32 [4, 3328], replicated
- grad_conv_bias: float32 [3328], replicated
- grad_dt_bias: float32 [48], replicated
- grad_a_log: float32 [48], replicated
- grad_skip_d: float32 [48], replicated
- grad_gnorm_gain: float32 [3072], replicated
- grad_out_weight: float32 [3072, 1536], P('shard')
The draws below stay inside these ranges and needn't reach their ends.
Inputs may be any that keep to these rules, and one draw needn't show every extreme that they name: `segment_ids`: segment ids never fall along a sequence; each document holds at most 128 tokens and one holds exactly that many.
All inputs are finite; a program needn't handle non-finite values.
Results may differ from the reference program's by a relative error of at most 0.0073.
Values may be sent and summed in bfloat16 or wider, within the bound.
No kernel may reach another device: no remote copies, remote signals or barrier semaphores. Data moves between devices by JAX's collectives and lax.ppermute only.
A program may use at most 256 MiB of HBM per device.

```python
import math
import jax
import jax.numpy as jnp
import numpy as np
from jax import lax

D = 1536
HEADS = 48
CONV = 4
SPAN = 256
LEN = 256
D_INNER = 3072
XBC = 3328
E = 6448
SEQS = 128
TOKENS = 32768


def levels(key, extent, cuts, low, largest):
    def one(dim, shards_of):
        draws = jax.random.uniform(jax.random.fold_in(jax.random.fold_in(key, 6), dim), (shards_of,), jnp.float32, low / len(cuts), largest / len(cuts))
        return jnp.repeat(jnp.exp(draws), extent[dim] // shards_of).reshape((-1,) + (1,) * (len(extent) - dim - 1))

    level = one(*cuts[0])
    for cut in cuts[1:]:
        level = level * one(*cut)
    return level


def split_up(count, total, limit, lean):
    loads = [(1 << 20) // math.isqrt(grade ** lean) + 1 for grade in range(2, count + 1)]
    rest, given = total - limit - (count - 1), [1] * (count - 1)
    while rest > 0:
        candidates = [i for i in range(count - 1) if given[i] < limit]
        whole, remaining = sum([loads[i] for i in candidates]), rest
        for i in candidates:
            extra = min(limit - given[i], max(1, remaining * loads[i] // whole), rest)
            given[i] = given[i] + extra
            rest = rest - extra
    return np.array([limit] + given)


def uneven_parts(rng, count, total, bound, slope):
    if count == 2:
        one = jax.random.randint(rng, (), max(1, total - bound), min(bound, total - 1) + 1)
        return jnp.stack([one, total - one])
    sizes = jnp.asarray(split_up(count, total, bound, slope), jnp.int32)
    couples = (count - 1) // 2
    giver, receiver = sizes[1:1 + 2 * couples:2], sizes[2:2 + 2 * couples:2]
    slack = jnp.minimum(giver - 1, bound - receiver)
    moved = jax.random.randint(jax.random.fold_in(rng, 1), (couples,), 0, 1 << 20) % (slack + 1)
    sizes = sizes.at[1:1 + 2 * couples:2].set(giver - moved).at[2:2 + 2 * couples:2].set(receiver + moved)
    return sizes[jax.random.permutation(jax.random.fold_in(rng, 2), count)]


def scatter_about(own_key, shape, width, reach, cuts=(), kind=jnp.bfloat16):
    factor_of = levels(own_key, shape, cuts, -0.22, 0.18) if cuts else 1.0
    drawn = jax.random.normal(own_key, shape, jnp.float32) * width * factor_of
    return jnp.minimum(jnp.maximum(drawn, -reach), reach).astype(kind)


def setup_inputs(seed: int = 0) -> dict:
    arg_keys = jax.random.split(jax.random.key(seed), 13)
    return {
        "tokens": scatter_about(arg_keys[0], (TOKENS, D), 1.0, 6.0, ((0, 128),)),
        "segment_ids": jax.vmap(lambda own: jnp.searchsorted(jnp.cumsum(uneven_parts(own, max(4, LEN // 32), LEN, LEN // 2, 2)), jnp.arange(LEN), side="right"))(jax.random.split(arg_keys[1], SEQS)).reshape((SEQS, LEN)).astype(jnp.int32),
        "norm_gain": jnp.clip(1.0 + 0.1 * jax.random.normal(arg_keys[2], (D,), jnp.float32), 0.5, 1.5),
        "in_weight": scatter_about(arg_keys[3], (D, E), D ** -0.5, 0.15625, ((0, 64),)),
        "conv_weight": scatter_about(arg_keys[4], (CONV, XBC), CONV ** -0.5, 3.0, (), jnp.float32),
        "conv_bias": scatter_about(arg_keys[5], (XBC,), 0.3, 2.0, (), jnp.float32),
        "dt_bias": jnp.clip(jax.random.uniform(arg_keys[6], (HEADS,), jnp.float32, -5.0, -2.0), -5.0, -2.0),
        "a_log": jnp.clip(jax.random.uniform(arg_keys[7], (HEADS,), jnp.float32, -0.5, 2.5), -0.5, 2.5),
        "skip_d": jnp.clip(jax.random.uniform(arg_keys[8], (HEADS,), jnp.float32, 0.5, 1.5), 0.5, 1.5),
        "gnorm_gain": jnp.clip(1.0 + 0.1 * jax.random.normal(arg_keys[9], (D_INNER,), jnp.float32), 0.5, 1.5),
        "out_weight": scatter_about(arg_keys[10], (D_INNER, D), D_INNER ** -0.5, 0.109375, ((0, 64),)),
        "cotangent": scatter_about(arg_keys[11], (TOKENS, D), 1.0, 6.0, ((0, 128),)),
    }


@jax.custom_vjp
def low(v):
    return lax.optimization_barrier(v.astype(jnp.bfloat16)).astype(jnp.float32)

@jax.custom_vjp
def low_back(v):
    return v

def low_keep(v):
    return (low(v), None)

def low_pass(kept, grad):
    return (grad,)

def back_keep(v):
    return (v, None)

def back_low(kept, grad):
    return (low(grad),)
low.defvjp(low_keep, low_pass)
low_back.defvjp(back_keep, back_low)
norm_eps = 1e-05
highest = lax.Precision.HIGHEST

def rms_gain(values, gain):
    return values * lax.rsqrt(lax.optimization_barrier(jnp.mean(values * values, axis=-1, keepdims=True)) + norm_eps) * gain

def block_step(carry, pieces):
    ssm_state, prev_doc = carry
    x_block, b_block, c_block, dt_block, rate_block, seg_block = pieces
    cumulative = jnp.cumsum(rate_block, axis=0)
    position = jnp.arange(seg_block.shape[0])
    causal_same = ((position[:, None] >= position[None, :]) & (seg_block[:, None] == seg_block[None, :])).astype(rate_block.dtype)
    log_gap = cumulative[:, None, :] - cumulative[None, :, :]
    decay_table = jnp.exp(jnp.where(causal_same[:, :, None] > 0, log_gap, 0.0)) * causal_same[:, :, None]
    scores = jnp.dot(c_block, b_block.T, precision=highest)
    weights = scores[:, :, None] * decay_table * dt_block[None, :, :]
    inside = jnp.einsum('tsh,shp->thp', weights, x_block, precision=highest)
    keep_state = (seg_block == prev_doc).astype(rate_block.dtype)
    from_state = jnp.einsum('tn,hpn->thp', c_block, ssm_state, precision=highest) * (keep_state[:, None] * jnp.exp(cumulative))[:, :, None]
    last_doc = seg_block[-1]
    tail_weight = jnp.exp(cumulative[-1][None, :] - cumulative) * dt_block * (seg_block == last_doc).astype(rate_block.dtype)[:, None]
    carried = (last_doc == prev_doc).astype(rate_block.dtype) * jnp.exp(cumulative[-1])[:, None, None] * ssm_state
    state_new = carried + jnp.einsum('sh,shp,sn->hpn', tail_weight, x_block, b_block, precision=highest)
    return ((state_new, last_doc), inside + from_state)

def mix_layer(projected, segments, conv_weight, conv_bias, dt_bias, a_log, skip_d, gnorm_gain):
    length = projected.shape[0]
    inner_width = gnorm_gain.shape[0]
    head_count = dt_bias.shape[0]
    head_dim = inner_width // head_count
    conv_width = conv_bias.shape[0]
    state_dim = (conv_width - inner_width) // 2
    tap_count = conv_weight.shape[0]
    gate_part = projected[:, :inner_width]
    conv_input = projected[:, inner_width:inner_width + conv_width]
    dt_raw = projected[:, inner_width + conv_width:]
    seg_padded = jnp.concatenate([jnp.full((tap_count - 1,), -1, jnp.int32), segments.astype(jnp.int32)])
    input_padded = jnp.concatenate([jnp.zeros((tap_count - 1, conv_width), projected.dtype), conv_input], axis=0)
    convolved = conv_bias + jnp.zeros_like(conv_input)
    for tap_index in range(tap_count):
        shifted = input_padded[tap_index:tap_index + length]
        same_doc = (seg_padded[tap_index:tap_index + length] == segments.astype(jnp.int32)).astype(projected.dtype)
        convolved = convolved + conv_weight[tap_index] * shifted * same_doc[:, None]
    activated = jax.nn.silu(convolved)
    x_heads = activated[:, :inner_width].reshape(length, head_count, head_dim)
    b_matrix = activated[:, inner_width:inner_width + state_dim]
    c_matrix = activated[:, inner_width + state_dim:]
    step_size = jax.nn.softplus(dt_raw + dt_bias)
    log_decay = -step_size * jnp.exp(a_log)
    block_count = length // SPAN
    pieces = (x_heads.reshape(block_count, SPAN, head_count, head_dim), b_matrix.reshape(block_count, SPAN, state_dim), c_matrix.reshape(block_count, SPAN, state_dim), step_size.reshape(block_count, SPAN, head_count), log_decay.reshape(block_count, SPAN, head_count), segments.astype(jnp.int32).reshape(block_count, SPAN))
    start_carry = (jnp.zeros((head_count, head_dim, state_dim), projected.dtype), jnp.array(-1, jnp.int32))
    ignored, block_out = lax.scan(jax.checkpoint(block_step), start_carry, pieces)
    mixed_out = block_out.reshape(length, head_count, head_dim) + skip_d[:, None] * x_heads
    gated_out = mixed_out.reshape(length, inner_width) * jax.nn.silu(gate_part)
    return rms_gain(gated_out, gnorm_gain)

def reference(tokens, segment_ids, norm_gain, in_weight, conv_weight, conv_bias, dt_bias, a_log, skip_d, gnorm_gain, out_weight, cotangent):

    def layer(tokens_full, gain_in, in_full, conv_taps, conv_shift, dt_shift, decay_log, skip_head, gain_gated, out_full):

        def one_sequence(inputs):
            rows, segments = inputs
            normed = rms_gain(rows, gain_in)
            projected = low_back(jnp.dot(low(normed), in_full, precision=highest))
            mixer_out = mix_layer(projected, segments, conv_taps, conv_shift, dt_shift, decay_log, skip_head, gain_gated)
            return rows + jnp.dot(low(mixer_out), out_full, precision=highest)
        outputs = lax.map(jax.checkpoint(one_sequence), (tokens_full.reshape(SEQS, LEN, D), segment_ids))
        return outputs.reshape(TOKENS, D)
    primals = (tokens.astype(jnp.float32), norm_gain.astype(jnp.float32), in_weight.astype(jnp.float32), conv_weight.astype(jnp.float32), conv_bias.astype(jnp.float32), dt_bias.astype(jnp.float32), a_log.astype(jnp.float32), skip_d.astype(jnp.float32), gnorm_gain.astype(jnp.float32), out_weight.astype(jnp.float32))
    outputs, backward = jax.vjp(layer, *primals)
    grads = backward(cotangent.astype(jnp.float32))
    return (outputs.astype(jnp.bfloat16), grads[0], grads[1], grads[2], grads[3], grads[4], grads[5], grads[6], grads[7], grads[8], grads[9])
```

```python
import functools

import jax
import jax.numpy as jnp
import numpy as np
from jax import lax
from jax.experimental import pallas as pl
from jax.experimental.pallas import tpu as pltpu
from jax.sharding import Mesh
from jax.sharding import PartitionSpec as P

LEN = 256
HALF = 128
HEAD = 64
GROUP = 8
WIDE = GROUP * HEAD
STATE = 128
TAPS = 4
NORM_EPS = 1e-05
LOG2E = 1.4426950408889634
FAR = -1e30
bf16 = jnp.bfloat16
f32 = jnp.float32
highest = lax.Precision.HIGHEST


def sigmoid(v):
    return 0.5 + 0.5 * jnp.tanh(0.5 * v)


def convolve(values, taps, bias, near):
    total = bias + taps[TAPS - 1 : TAPS] * values
    for back in range(1, TAPS):
        tap = taps[TAPS - 1 - back : TAPS - back]
        total = total + tap * (near[:, back : back + 1] * pltpu.roll(values, back, 0))
    return total


def convolve_back(grad, values, taps, near):
    total = taps[TAPS - 1 : TAPS] * grad
    rows = [jnp.sum(grad * values, axis=0, keepdims=True)]
    for back in range(1, TAPS):
        tap = taps[TAPS - 1 - back : TAPS - back]
        seen = near[:, back : back + 1] * grad
        total = total + tap * pltpu.roll(seen, LEN - back, 0)
        rows.append(jnp.sum(seen * pltpu.roll(values, back, 0), axis=0, keepdims=True))
    return total, rows[::-1] + [jnp.sum(grad, axis=0, keepdims=True)]


def silu_slope(v, s):
    return s * (1.0 + v * (1.0 - s))


def positions():
    return (
        lax.broadcasted_iota(jnp.int32, (LEN, LEN), 0),
        lax.broadcasted_iota(jnp.int32, (LEN, LEN), 1),
    )


def softplus(v):
    small = jnp.exp(-jnp.abs(v))
    return jnp.maximum(v, 0.0) + jnp.log1p(small)


def steps_of(dt_part, head_rows):
    raw = dt_part + head_rows[0:1]
    step = softplus(raw)
    rate = -step * head_rows[1:2]
    row, col = positions()
    lower = (row >= col).astype(f32)
    total = jnp.dot(lower, rate, precision=highest, preferred_element_type=f32) * LOG2E
    return raw, step, rate, total


def split_dot(values, ones):
    high = values.astype(bf16)
    low = (values - high.astype(f32)).astype(bf16)
    return jnp.dot(high, ones, preferred_element_type=f32) + jnp.dot(
        low, ones, preferred_element_type=f32
    )


def pair_columns(table, pair):
    lane = lax.broadcasted_iota(jnp.int32, (LEN, 2 * HEAD), 1)
    return jnp.where(lane < HEAD, table[:, 2 * pair : 2 * pair + 1], table[:, 2 * pair + 1 : 2 * pair + 2])


def halves(values):
    lane = lax.broadcasted_iota(jnp.int32, values.shape, 1)
    zero = jnp.zeros_like(values)
    return jnp.where(lane < HEAD, values, zero), jnp.where(lane >= HEAD, values, zero)


def mix_forward_kernel(
    proj_ref, shared_ref, near_ref, seg_col_ref, seg_row_ref, taps_ref, taps_shared_ref, head_ref,
    ssd_ref, scores, apart, totals, totals_row, steps,
):
    group = pl.program_id(1)
    near = near_ref[...]

    @pl.when(group == 0)
    def _():
        shared = shared_ref[...]
        mixed = convolve(shared[:, : 2 * STATE], taps_shared_ref[0:4], taps_shared_ref[4:5], near)
        mixed = mixed * sigmoid(mixed)
        b_low = mixed[:, :STATE].astype(bf16)
        c_low = mixed[:, STATE:].astype(bf16)
        scores[...] = lax.dot_general(
            c_low, b_low, (((1,), (1,)), ((), ())), preferred_element_type=f32
        )
        row, col = positions()
        seen = (row >= col) & (seg_col_ref[...] == seg_row_ref[0])
        apart[...] = jnp.where(seen, 0.0, FAR)
        raw, step, rate, total = steps_of(shared[:, 2 * STATE :], head_ref[...])
        for g in range(totals.shape[0]):
            turn = (STATE - GROUP * g) % STATE
            totals[g] = pltpu.roll(total, turn, 1) if turn else total
            steps[g] = pltpu.roll(step, turn, 1) if turn else step
        totals_row[...] = total.T

    values = proj_ref[...]
    mixed = convolve(values, taps_ref[0:4], taps_ref[4:5], near)
    x = mixed * sigmoid(mixed)
    total = totals[group]
    step = steps[group]
    total_row = totals_row[pl.ds(pl.multiple_of(group * GROUP, GROUP), GROUP), :]
    skip = taps_ref[5:6]
    for pair in range(GROUP // 2):
        lanes = slice(2 * HEAD * pair, 2 * HEAD * (pair + 1))
        x_pair = x[:, lanes]
        sides = halves((pair_columns(step, pair) * x_pair).astype(bf16))
        upper = lower = 0.0
        for side in range(2):
            head = 2 * pair + side
            col = total[:, head : head + 1]
            row = total_row[head : head + 1, :]
            decay = jnp.exp2(col[:HALF] - row[:, :HALF] + apart[:HALF, :HALF])
            weight = (scores[:HALF, :HALF] * decay).astype(bf16)
            upper = upper + jnp.dot(weight, sides[side][:HALF], preferred_element_type=f32)
            decay = jnp.exp2(col[HALF:] - row + apart[HALF:, :])
            weight = (scores[HALF:, :] * decay).astype(bf16)
            lower = lower + jnp.dot(weight, sides[side], preferred_element_type=f32)
        skipped = skip[:, lanes] * x_pair
        ssd_ref[:HALF, lanes] = upper + skipped[:HALF]
        ssd_ref[HALF:, lanes] = lower + skipped[HALF:]


def mix_backward_kernel(
    proj_ref, shared_ref, near_ref, seg_col_ref, seg_row_ref, taps_ref, taps_shared_ref, head_ref,
    ssd_ref, dssd_ref,
    dproj_ref, drows_ref, drows_shared_ref, dheads_ref,
    scores, apart, totals, totals_row, steps, b_keep, c_keep, dscores, dtotal, dstep,
):
    group = pl.program_id(1)
    last = pl.num_programs(1) - 1
    near = near_ref[...]

    @pl.when(group == 0)
    def _():
        shared = shared_ref[...]
        mixed = convolve(shared[:, : 2 * STATE], taps_shared_ref[0:4], taps_shared_ref[4:5], near)
        mixed = mixed * sigmoid(mixed)
        b_low = mixed[:, :STATE].astype(bf16)
        c_low = mixed[:, STATE:].astype(bf16)
        b_keep[...] = b_low
        c_keep[...] = c_low
        scores[...] = lax.dot_general(
            b_low, c_low, (((1,), (1,)), ((), ())), preferred_element_type=f32
        )
        row, col = positions()
        seen = (row <= col) & (seg_col_ref[...] == seg_row_ref[0])
        apart[...] = jnp.where(seen, 0.0, FAR)
        raw, step, rate, total = steps_of(shared[:, 2 * STATE :], head_ref[...])
        for g in range(totals.shape[0]):
            turn = (STATE - GROUP * g) % STATE
            totals[g] = pltpu.roll(total, turn, 1) if turn else total
            steps[g] = pltpu.roll(step, turn, 1) if turn else step
        totals_row[...] = total.T
        dscores[...] = jnp.zeros_like(dscores)
        dtotal[...] = jnp.zeros_like(dtotal)
        dstep[...] = jnp.zeros_like(dstep)

    values = proj_ref[...]
    mixed = convolve(values, taps_ref[0:4], taps_ref[4:5], near)
    gate = sigmoid(mixed)
    x = mixed * gate
    total = totals[group]
    step = steps[group]
    total_row = totals_row[pl.ds(pl.multiple_of(group * GROUP, GROUP), GROUP), :]
    skip = taps_ref[5:6]
    dx_parts, total_parts, step_parts, skip_parts = [], [], [], []
    for pair in range(GROUP // 2):
        lanes = slice(2 * HEAD * pair, 2 * HEAD * (pair + 1))
        x_pair = x[:, lanes]
        dt_pair = pair_columns(step, pair)
        low_x = (dt_pair * x_pair).astype(bf16)
        low_dy = dssd_ref[:, lanes]
        dy = low_dy.astype(f32)
        x_sides = halves(low_x)
        dy_sides = halves(low_dy)
        upper = lower = 0.0
        for side in range(2):
            head = 2 * pair + side
            col = total[:, head : head + 1]
            row = total_row[head : head + 1, :]
            decay = jnp.exp2(row - col[:HALF] + apart[:HALF, :])
            weight = (scores[:HALF, :] * decay).astype(bf16)
            upper = upper + jnp.dot(weight, dy_sides[side], preferred_element_type=f32)
            grad = lax.dot_general(
                x_sides[side][:HALF], low_dy, (((1,), (1,)), ((), ())), preferred_element_type=f32
            )
            dscores[:HALF, :] += grad * decay
            decay = jnp.exp2(row[:, HALF:] - col[HALF:] + apart[HALF:, HALF:])
            weight = (scores[HALF:, HALF:] * decay).astype(bf16)
            lower = lower + jnp.dot(weight, dy_sides[side][HALF:], preferred_element_type=f32)
            grad = lax.dot_general(
                x_sides[side][HALF:], low_dy[HALF:], (((1,), (1,)), ((), ())),
                preferred_element_type=f32,
            )
            dscores[HALF:, HALF:] += grad * decay
        back = jnp.concatenate([upper, lower], axis=0)
        skip_pair = skip[:, lanes]
        inside = ssd_ref[:, lanes] - skip_pair * x_pair
        total_parts.append(dy * inside - low_x.astype(f32) * back)
        step_parts.append(x_pair * back)
        skip_parts.append(jnp.sum(dy * x_pair, axis=0, keepdims=True))
        dx_parts.append(dt_pair * back + skip_pair * dy)
    wide = lambda parts: jnp.concatenate(parts, axis=1)
    place = lax.broadcasted_iota(jnp.int32, (WIDE, STATE), 0) // HEAD + group * GROUP
    ones = (place == lax.broadcasted_iota(jnp.int32, (WIDE, STATE), 1)).astype(bf16)
    dtotal[...] += split_dot(wide(total_parts), ones)
    dstep[...] += split_dot(wide(step_parts), ones)
    dmixed = wide(dx_parts) * silu_slope(mixed, gate)
    dvalues, rows = convolve_back(dmixed, values, taps_ref[0:4], near)
    dproj_ref[:, pl.ds(pl.multiple_of(group * WIDE, WIDE), WIDE)] = dvalues.astype(bf16)
    drows_ref[0] = jnp.concatenate(
        rows + [wide(skip_parts), jnp.zeros((2, WIDE), f32)], axis=0
    )

    @pl.when(group == last)
    def _():
        shared = shared_ref[...]
        values = shared[:, : 2 * STATE]
        mixed = convolve(values, taps_shared_ref[0:4], taps_shared_ref[4:5], near)
        gate = sigmoid(mixed)
        low = dscores[...].astype(bf16)
        db = jnp.dot(low, c_keep[...], preferred_element_type=f32)
        dc = lax.dot_general(
            low, b_keep[...], (((0,), (0,)), ((), ())), preferred_element_type=f32
        )
        dmixed = jnp.concatenate([db, dc], axis=1) * silu_slope(mixed, gate)
        dvalues, rows = convolve_back(dmixed, values, taps_shared_ref[0:4], near)
        drows_shared_ref[0] = jnp.concatenate(rows + [jnp.zeros((3, 2 * STATE), f32)], axis=0)
        raw, step, rate, total = steps_of(shared[:, 2 * STATE :], head_ref[...])
        row, col = positions()
        upper = (row <= col).astype(f32)
        drate = jnp.dot(upper, dtotal[...], precision=highest, preferred_element_type=f32)
        draw = (dstep[...] - drate * head_ref[1:2]) * sigmoid(raw)
        at = dproj_ref.shape[1] - 3 * STATE
        dproj_ref[:, at : at + 2 * STATE] = dvalues.astype(bf16)
        dproj_ref[:, at + 2 * STATE :] = draw.astype(bf16)
        dheads_ref[0] = jnp.concatenate(
            [
                jnp.sum(draw, axis=0, keepdims=True),
                jnp.sum(drate * rate, axis=0, keepdims=True),
                jnp.zeros((6, STATE), f32),
            ],
            axis=0,
        )


def mixer_specs(columns):
    return [
        pl.BlockSpec((LEN, WIDE), lambda s, g: (s, g)),
        pl.BlockSpec((LEN, 3 * STATE), lambda s, g: (s, columns // (3 * STATE))),
        pl.BlockSpec((LEN, 8), lambda s, g: (s, 0)),
        pl.BlockSpec((LEN, 1), lambda s, g: (s, 0)),
        pl.BlockSpec((1, 1, LEN), lambda s, g: (s, 0, 0)),
        pl.BlockSpec((8, WIDE), lambda s, g: (0, g)),
        pl.BlockSpec((8, 2 * STATE), lambda s, g: (0, 0)),
        pl.BlockSpec((8, STATE), lambda s, g: (0, 0)),
    ]


def mixer_scratch(groups):
    return [
        pltpu.VMEM((LEN, LEN), f32),
        pltpu.VMEM((LEN, LEN), f32),
        pltpu.VMEM((groups, LEN, STATE), f32),
        pltpu.VMEM((STATE, LEN), f32),
        pltpu.VMEM((groups, LEN, STATE), f32),
    ]


def mix_forward(proj, near, seg_col, seg_row, taps, taps_shared, heads):
    rows, columns = proj.shape[0], proj.shape[1] - 3 * STATE
    groups = columns // WIDE
    return pl.pallas_call(
        mix_forward_kernel,
        grid=(rows // LEN, groups),
        in_specs=mixer_specs(columns),
        out_specs=pl.BlockSpec((LEN, WIDE), lambda s, g: (s, g)),
        out_shape=jax.ShapeDtypeStruct((rows, columns), f32),
        scratch_shapes=mixer_scratch(groups),
        compiler_params=pltpu.CompilerParams(vmem_limit_bytes=32 * 2**20),
        cost_estimate=pl.CostEstimate(flops=10**9, bytes_accessed=8 * 2**20, transcendentals=10**7),
        name="mix_forward",
    )(proj, proj, near, seg_col, seg_row, taps, taps_shared, heads)


def mix_backward(proj, near, seg_col, seg_row, taps, taps_shared, heads, ssd, dssd):
    rows, columns = proj.shape[0], proj.shape[1] - 3 * STATE
    groups, seqs = columns // WIDE, rows // LEN
    wide = pl.BlockSpec((LEN, WIDE), lambda s, g: (s, g))
    return pl.pallas_call(
        mix_backward_kernel,
        grid=(seqs, groups),
        in_specs=mixer_specs(columns) + [wide, wide],
        out_specs=[
            pl.BlockSpec((LEN, columns + 3 * STATE), lambda s, g: (s, 0)),
            pl.BlockSpec((1, 8, WIDE), lambda s, g: (s, 0, g)),
            pl.BlockSpec((1, 8, 2 * STATE), lambda s, g: (s, 0, 0)),
            pl.BlockSpec((1, 8, STATE), lambda s, g: (s, 0, 0)),
        ],
        out_shape=[
            jax.ShapeDtypeStruct(proj.shape, bf16),
            jax.ShapeDtypeStruct((seqs, 8, columns), f32),
            jax.ShapeDtypeStruct((seqs, 8, 2 * STATE), f32),
            jax.ShapeDtypeStruct((seqs, 8, STATE), f32),
        ],
        scratch_shapes=mixer_scratch(groups)
        + [
            pltpu.VMEM((LEN, STATE), bf16),
            pltpu.VMEM((LEN, STATE), bf16),
            pltpu.VMEM((LEN, LEN), f32),
            pltpu.VMEM((LEN, STATE), f32),
            pltpu.VMEM((LEN, STATE), f32),
        ],
        compiler_params=pltpu.CompilerParams(vmem_limit_bytes=40 * 2**20),
        cost_estimate=pl.CostEstimate(flops=3 * 10**9, bytes_accessed=12 * 2**20, transcendentals=10**7),
        name="mix_backward",
    )(proj, proj, near, seg_col, seg_row, taps, taps_shared, heads, ssd, dssd)


def shifted(value, axis, by):
    size = lax.axis_size(axis)
    return lax.ppermute(value, axis, [(i, (i + by) % size) for i in range(size)])


def swapped(value):
    return lax.ppermute(value, "grp", [(0, 1), (1, 0)])


def in_order(own, other, axis=0):
    first = lax.axis_index("grp") == 0
    return jnp.concatenate([jnp.where(first, own, other), jnp.where(first, other, own)], axis=axis)


def turned(value, dim, by):
    twice = jnp.concatenate([value, value], axis=dim)
    return lax.dynamic_slice_in_dim(twice, by, value.shape[dim], dim)


def summed_over(value, axis):
    total = value
    for by in range(1, lax.axis_size(axis)):
        total = total + shifted(value, axis, by)
    return total


def scattered(pieces, axis):
    total = pieces[0]
    for by in range(1, len(pieces)):
        total = total + shifted(pieces[by].astype(bf16), axis, by).astype(f32)
    return total


def halved(array, size, dim):
    return lax.dynamic_slice_in_dim(array, lax.axis_index("grp") * size, size, dim)


def times(left, right):
    return jnp.dot(left, right, preferred_element_type=f32)


def times_turned(left, right):
    return lax.dot_general(left, right, (((1,), (1,)), ((), ())), preferred_element_type=f32)


CHIPS = ("z", "y", "x")
ORDERS = (("z", "y", "x"), ("y", "x", "z"), ("x", "z", "y"))


def on_device(
    tokens,
    segment_ids,
    norm_gain,
    in_weight,
    conv_weight,
    conv_bias,
    dt_bias,
    a_log,
    skip_d,
    gnorm_gain,
    out_weight,
    cotangent,
):
    width = tokens.shape[1]
    inner = gnorm_gain.shape[0]
    half = inner // 2
    heads = dt_bias.shape[0] // 2
    bc = conv_bias.shape[0] - inner
    rows_in, rows_out = in_weight.shape[0], out_weight.shape[0]

    w_dt = halved(in_weight[:, inner + inner + bc :], heads, 1)
    own_mix = jnp.concatenate(
        [
            halved(in_weight[:, inner : 2 * inner], half, 1),
            in_weight[:, 2 * inner : 2 * inner + bc],
            w_dt,
            jnp.zeros((rows_in, STATE - heads), bf16),
        ],
        axis=1,
    )
    own_gate = halved(in_weight[:, :inner], half, 1)
    own_out = halved(out_weight, width // 2, 1)
    w_mix = lax.all_gather(own_mix, CHIPS, axis=0, tiled=True)
    w_gate = lax.all_gather(own_gate, CHIPS, axis=0, tiled=True)
    w_out = lax.all_gather(own_out, CHIPS, axis=0, tiled=True)

    residual = tokens.astype(f32)
    scale = lax.rsqrt(jnp.mean(residual * residual, axis=-1, keepdims=True) + NORM_EPS)
    unit = residual * scale
    own_low = (unit * norm_gain).astype(bf16)
    normed = in_order(own_low, swapped(own_low))
    cot = in_order(cotangent, swapped(cotangent))
    segments = in_order(segment_ids, swapped(segment_ids))
    near = [jnp.zeros(segments.shape, f32)]
    for back in range(1, TAPS):
        same = (segments[:, back:] == segments[:, :-back]).astype(f32)
        near.append(jnp.pad(same, ((0, 0), (back, 0))))
    near = jnp.stack(near + [near[0]] * 4, axis=-1).reshape(-1, 8)
    seg_col = segments.astype(f32).reshape(-1, 1)
    seg_row = segments.astype(f32)[:, None, :]

    taps = jnp.concatenate(
        [
            halved(conv_weight[:, :inner], half, 1),
            halved(conv_bias[None, :inner], half, 1),
            jnp.repeat(halved(skip_d, heads, 0), HEAD)[None],
            jnp.zeros((2, half), f32),
        ]
    )
    taps_shared = jnp.concatenate(
        [conv_weight[:, inner:], conv_bias[None, inner:], jnp.zeros((3, bc), f32)]
    )
    head_rows = jnp.stack([halved(dt_bias, heads, 0), jnp.exp(halved(a_log, heads, 0))])
    head_rows = jnp.pad(head_rows, ((0, 6), (0, STATE - heads)))
    gain = halved(gnorm_gain, half, 0)

    turned_low = normed.T.reshape(4, 4, 4, rows_in, -1)
    for dim, axis in enumerate(CHIPS):
        turned_low = turned(turned_low, dim, lax.axis_index(axis))
    leaving = []
    for order in ORDERS:
        dims = tuple(CHIPS.index(axis) for axis in order)
        leaving.append(turned_low.transpose(dims + (3, 4)).reshape(4, 16 * rows_in, -1))

    proj = times(normed, w_mix)
    sides = (near, seg_col, seg_row, taps, taps_shared, head_rows)
    ssd = mix_forward(proj, *sides)
    gate_part = times(normed, w_gate)
    cot_half = halved(cot, width // 2, 1)
    mixer_parts = times_turned(cot_half, w_out).astype(bf16)
    core = lax.axis_index("grp")
    grad_mixer = halved(mixer_parts, half, 1).astype(f32) + swapped(
        lax.dynamic_slice_in_dim(mixer_parts, (1 - core) * half, half, 1)
    ).astype(f32)
    opened = sigmoid(gate_part)
    gate = gate_part * opened
    gated = ssd * gate
    weighted = grad_mixer * gain
    sums = jnp.stack([jnp.sum(gated * gated, axis=-1), jnp.sum(gated * weighted, axis=-1)])
    sums = sums + swapped(sums)
    gscale = lax.rsqrt(sums[0] / inner + NORM_EPS)[:, None]
    pull = gscale * gscale * gscale * (sums[1] / inner)[:, None]
    mixer_low = (gated * gscale * gain).astype(bf16)
    dgated = gscale * weighted - gated * pull
    grad_gain = jnp.sum(grad_mixer * gated * gscale, axis=0)
    dgate_low = (dgated * ssd * silu_slope(gate_part, opened)).astype(bf16)
    dssd = (dgated * gate).astype(bf16)
    mixer_other = swapped(mixer_low)
    mixer_all = in_order(mixer_low, mixer_other, axis=1)

    out_grad = lax.dot_general(
        mixer_all, cot_half, (((0,), (0,)), ((), ())), preferred_element_type=f32
    ).astype(bf16)
    gate_grad = times(normed.T, dgate_low).astype(bf16)
    out_share = lax.psum_scatter(out_grad, ("z", "y"), scatter_dimension=0, tiled=True)
    gate_share = lax.psum_scatter(gate_grad, ("z", "y"), scatter_dimension=0, tiled=True)

    dproj, drows, drows_shared, dheads = mix_backward(proj, *sides, ssd, dssd)
    mix_shares = []
    wide = dproj.shape[1] // 3
    for stream, order in enumerate(ORDERS):
        columns = dproj[:, stream * wide : (stream + 1) * wide]
        pieces = [times(leaving[stream][k], columns) for k in range(4)]
        share = scattered(pieces, order[0])
        share = scattered(list(share.reshape(4, 4 * rows_in, wide)), order[1])
        share = scattered(list(share.reshape(4, rows_in, wide)), order[2])
        mix_shares.append(share)
    mix_share = jnp.concatenate(mix_shares, axis=1)

    out_turned = turned(out_share.reshape(4, rows_out, -1), 0, lax.axis_index("x"))
    out_total = scattered([out_turned[0].astype(f32)] + list(out_turned[1:]), "x")
    gate_turned = turned(gate_share.reshape(4, rows_in, -1), 0, lax.axis_index("x"))
    gate_total = scattered([gate_turned[0].astype(f32)] + list(gate_turned[1:]), "x")

    out_part = times(mixer_all, w_out)
    out_own = halved(out_part, LEN, 0).astype(bf16)
    out_other = swapped(lax.dynamic_slice_in_dim(out_part, (1 - core) * LEN, LEN, 0).astype(bf16))
    branch = in_order(out_own, out_other, axis=1)
    out_tokens = (residual + branch.astype(f32)).astype(bf16)

    normed_part = times_turned(dproj, w_mix) + times_turned(dgate_low, w_gate)
    grad_normed = halved(normed_part, LEN, 0) + swapped(
        lax.dynamic_slice_in_dim(normed_part, (1 - core) * LEN, LEN, 0).astype(bf16)
    ).astype(f32)
    q = grad_normed * norm_gain
    grad_tokens = cotangent.astype(f32) + scale * (
        q - unit * jnp.mean(q * unit, axis=-1, keepdims=True)
    )
    grad_norm_gain = jnp.sum(grad_normed * unit, axis=0)

    drows, drows_shared, dheads = drows.sum(0), drows_shared.sum(0), dheads.sum(0)
    small = jnp.concatenate(
        [
            drows[:6],
            grad_gain[None],
            grad_norm_gain[None],
            jnp.concatenate([drows_shared[:5].reshape(1, -1), dheads[:2].reshape(1, -1)], axis=1),
        ]
    )
    for axis in CHIPS:
        small = summed_over(small, axis)

    small_other = swapped(small)
    mix_other, gate_other, out_other = swapped(mix_share), swapped(gate_total), swapped(out_total)
    bc_sum = (mix_share + mix_other)[:, half : half + bc]
    dt_at = slice(half + bc, half + bc + heads)
    grad_in_weight = jnp.concatenate(
        [
            in_order(gate_total, gate_other, axis=1),
            in_order(mix_share[:, :half], mix_other[:, :half], axis=1),
            bc_sum,
            in_order(mix_share[:, dt_at], mix_other[:, dt_at], axis=1),
        ],
        axis=1,
    )
    grad_out_weight = in_order(out_total, out_other, axis=1)
    both = in_order(small[:7], small_other[:7], axis=1)
    shared_sum = (small + small_other)[7:]
    shared_rows = shared_sum[1, : 5 * bc].reshape(5, bc)
    head_sums = in_order(
        small[8, 5 * bc :].reshape(2, STATE)[:, :heads],
        small_other[8, 5 * bc :].reshape(2, STATE)[:, :heads],
        axis=1,
    )
    return (
        out_tokens,
        grad_tokens,
        shared_sum[0],
        grad_in_weight,
        jnp.concatenate([both[:4], shared_rows[:4]], axis=1),
        jnp.concatenate([both[4], shared_rows[4]]),
        head_sums[0],
        head_sums[1],
        both[5].reshape(-1, HEAD).sum(axis=-1),
        both[6],
        grad_out_weight,
    )


def solution(mesh):
    chips = Mesh(mesh.devices.reshape(2, 4, 4, 4), ("grp",) + CHIPS)
    rows = P(("grp",) + CHIPS, None)
    owned = P(CHIPS, None)
    return jax.shard_map(
        on_device,
        mesh=chips,
        in_specs=(rows, rows, P(), owned, P(), P(), P(), P(), P(), P(), owned, rows),
        out_specs=(rows, rows, P(), owned, P(), P(), P(), P(), P(), P(), owned),
        check_vma=False,
    )
```

```python
import functools

import jax
import jax.numpy as jnp
import numpy as np
from jax import lax
from jax.experimental import pallas as pl
from jax.experimental.pallas import tpu as pltpu
from jax.sharding import Mesh
from jax.sharding import PartitionSpec as P

LEN = 256
VMEM = 24 * 2**20
HALF = 128
HEAD = 64
GROUP = 8
WIDE = GROUP * HEAD
STATE = 128
TAPS = 4
NORM_EPS = 1e-05
LOG2E = 1.4426950408889634
FAR = -1e30
bf16 = jnp.bfloat16
f32 = jnp.float32
highest = lax.Precision.HIGHEST


def sigmoid(v):
    return 0.5 + 0.5 * jnp.tanh(0.5 * v)


def convolve(values, taps, bias, near):
    total = bias + taps[TAPS - 1 : TAPS] * values
    for back in range(1, TAPS):
        tap = taps[TAPS - 1 - back : TAPS - back]
        total = total + tap * (near[:, back : back + 1] * pltpu.roll(values, back, 0))
    return total


def convolve_back(grad, values, taps, near):
    total = taps[TAPS - 1 : TAPS] * grad
    rows = [jnp.sum(grad * values, axis=0, keepdims=True)]
    for back in range(1, TAPS):
        tap = taps[TAPS - 1 - back : TAPS - back]
        seen = near[:, back : back + 1] * grad
        total = total + tap * pltpu.roll(seen, LEN - back, 0)
        rows.append(jnp.sum(seen * pltpu.roll(values, back, 0), axis=0, keepdims=True))
    return total, rows[::-1] + [jnp.sum(grad, axis=0, keepdims=True)]


def silu_slope(v, s):
    return s * (1.0 + v * (1.0 - s))


def positions():
    return (
        lax.broadcasted_iota(jnp.int32, (LEN, LEN), 0),
        lax.broadcasted_iota(jnp.int32, (LEN, LEN), 1),
    )


def softplus(v):
    small = jnp.exp(-jnp.abs(v))
    return jnp.maximum(v, 0.0) + jnp.log1p(small)


def steps_of(dt_part, head_rows):
    raw = dt_part + head_rows[0:1]
    step = softplus(raw)
    rate = -step * head_rows[1:2]
    row, col = positions()
    lower = (row >= col).astype(f32)
    total = jnp.dot(lower, rate, precision=highest, preferred_element_type=f32) * LOG2E
    return raw, step, rate, total


def split_dot(values, ones):
    high = values.astype(bf16)
    low = (values - high.astype(f32)).astype(bf16)
    return jnp.dot(high, ones, preferred_element_type=f32) + jnp.dot(
        low, ones, preferred_element_type=f32
    )


def pair_columns(table, pair):
    lane = lax.broadcasted_iota(jnp.int32, (LEN, 2 * HEAD), 1)
    return jnp.where(lane < HEAD, table[:, 2 * pair : 2 * pair + 1], table[:, 2 * pair + 1 : 2 * pair + 2])


def halves(values):
    lane = lax.broadcasted_iota(jnp.int32, values.shape, 1)
    zero = jnp.zeros_like(values)
    return jnp.where(lane < HEAD, values, zero), jnp.where(lane >= HEAD, values, zero)


def mix_forward_kernel(
    proj_ref, shared_ref, near_ref, seg_col_ref, seg_row_ref, taps_ref, taps_shared_ref, head_ref,
    ssd_ref, scores, apart, totals, totals_row, steps,
):
    group = pl.program_id(1)
    near = near_ref[...]

    @pl.when(group == 0)
    def _():
        shared = shared_ref[...]
        mixed = convolve(shared[:, : 2 * STATE], taps_shared_ref[0:4], taps_shared_ref[4:5], near)
        mixed = mixed * sigmoid(mixed)
        b_low = mixed[:, :STATE].astype(bf16)
        c_low = mixed[:, STATE:].astype(bf16)
        scores[...] = lax.dot_general(
            c_low, b_low, (((1,), (1,)), ((), ())), preferred_element_type=f32
        )
        row, col = positions()
        seen = (row >= col) & (seg_col_ref[...] == seg_row_ref[0])
        apart[...] = jnp.where(seen, 0.0, FAR)
        raw, step, rate, total = steps_of(shared[:, 2 * STATE :], head_ref[...])
        for g in range(totals.shape[0]):
            turn = (STATE - GROUP * g) % STATE
            totals[g] = pltpu.roll(total, turn, 1) if turn else total
            steps[g] = pltpu.roll(step, turn, 1) if turn else step
        totals_row[...] = total.T

    values = proj_ref[...]
    mixed = convolve(values, taps_ref[0:4], taps_ref[4:5], near)
    x = mixed * sigmoid(mixed)
    total = totals[group]
    step = steps[group]
    total_row = totals_row[pl.ds(pl.multiple_of(group * GROUP, GROUP), GROUP), :]
    skip = taps_ref[5:6]
    for pair in range(GROUP // 2):
        lanes = slice(2 * HEAD * pair, 2 * HEAD * (pair + 1))
        x_pair = x[:, lanes]
        sides = halves((pair_columns(step, pair) * x_pair).astype(bf16))
        upper = lower = 0.0
        for side in range(2):
            head = 2 * pair + side
            col = total[:, head : head + 1]
            row = total_row[head : head + 1, :]
            decay = jnp.exp2(col[:HALF] - row[:, :HALF] + apart[:HALF, :HALF])
            weight = (scores[:HALF, :HALF] * decay).astype(bf16)
            upper = upper + jnp.dot(weight, sides[side][:HALF], preferred_element_type=f32)
            decay = jnp.exp2(col[HALF:] - row + apart[HALF:, :])
            weight = (scores[HALF:, :] * decay).astype(bf16)
            lower = lower + jnp.dot(weight, sides[side], preferred_element_type=f32)
        skipped = skip[:, lanes] * x_pair
        ssd_ref[:HALF, lanes] = upper + skipped[:HALF]
        ssd_ref[HALF:, lanes] = lower + skipped[HALF:]


def mix_backward_kernel(
    proj_ref, shared_ref, near_ref, seg_col_ref, seg_row_ref, taps_ref, taps_shared_ref, head_ref,
    ssd_ref, dssd_ref,
    dproj_ref, drows_ref,
    scores, apart, totals, totals_row, steps, b_keep, c_keep, dscores, dtotal, dstep,
):
    group = pl.program_id(1)
    last = pl.num_programs(1) - 1
    near = near_ref[...]

    @pl.when(group == 0)
    def _():
        shared = shared_ref[...]
        mixed = convolve(shared[:, : 2 * STATE], taps_shared_ref[0:4], taps_shared_ref[4:5], near)
        mixed = mixed * sigmoid(mixed)
        b_low = mixed[:, :STATE].astype(bf16)
        c_low = mixed[:, STATE:].astype(bf16)
        b_keep[...] = b_low
        c_keep[...] = c_low
        scores[...] = lax.dot_general(
            b_low, c_low, (((1,), (1,)), ((), ())), preferred_element_type=f32
        )
        row, col = positions()
        seen = (row <= col) & (seg_col_ref[...] == seg_row_ref[0])
        apart[...] = jnp.where(seen, 0.0, FAR)
        raw, step, rate, total = steps_of(shared[:, 2 * STATE :], head_ref[...])
        for g in range(totals.shape[0]):
            turn = (STATE - GROUP * g) % STATE
            totals[g] = pltpu.roll(total, turn, 1) if turn else total
            steps[g] = pltpu.roll(step, turn, 1) if turn else step
        totals_row[...] = total.T
        dscores[...] = jnp.zeros_like(dscores)
        dtotal[...] = jnp.zeros_like(dtotal)
        dstep[...] = jnp.zeros_like(dstep)

    values = proj_ref[...]
    mixed = convolve(values, taps_ref[0:4], taps_ref[4:5], near)
    gate = sigmoid(mixed)
    x = mixed * gate
    total = totals[group]
    step = steps[group]
    total_row = totals_row[pl.ds(pl.multiple_of(group * GROUP, GROUP), GROUP), :]
    skip = taps_ref[5:6]
    dx_parts, total_parts, step_parts, skip_parts = [], [], [], []
    for pair in range(GROUP // 2):
        lanes = slice(2 * HEAD * pair, 2 * HEAD * (pair + 1))
        x_pair = x[:, lanes]
        dt_pair = pair_columns(step, pair)
        low_x = (dt_pair * x_pair).astype(bf16)
        low_dy = dssd_ref[:, lanes]
        dy = low_dy.astype(f32)
        x_sides = halves(low_x)
        dy_sides = halves(low_dy)
        upper = lower = 0.0
        for side in range(2):
            head = 2 * pair + side
            col = total[:, head : head + 1]
            row = total_row[head : head + 1, :]
            decay = jnp.exp2(row - col[:HALF] + apart[:HALF, :])
            weight = (scores[:HALF, :] * decay).astype(bf16)
            upper = upper + jnp.dot(weight, dy_sides[side], preferred_element_type=f32)
            grad = lax.dot_general(
                x_sides[side][:HALF], low_dy, (((1,), (1,)), ((), ())), preferred_element_type=f32
            )
            dscores[:HALF, :] += grad * decay
            decay = jnp.exp2(row[:, HALF:] - col[HALF:] + apart[HALF:, HALF:])
            weight = (scores[HALF:, HALF:] * decay).astype(bf16)
            lower = lower + jnp.dot(weight, dy_sides[side][HALF:], preferred_element_type=f32)
            grad = lax.dot_general(
                x_sides[side][HALF:], low_dy[HALF:], (((1,), (1,)), ((), ())),
                preferred_element_type=f32,
            )
            dscores[HALF:, HALF:] += grad * decay
        back = jnp.concatenate([upper, lower], axis=0)
        skip_pair = skip[:, lanes]
        inside = ssd_ref[:, lanes] - skip_pair * x_pair
        total_parts.append(dy * inside - low_x.astype(f32) * back)
        step_parts.append(x_pair * back)
        skip_parts.append(jnp.sum(dy * x_pair, axis=0, keepdims=True))
        dx_parts.append(dt_pair * back + skip_pair * dy)
    wide = lambda parts: jnp.concatenate(parts, axis=1)
    place = lax.broadcasted_iota(jnp.int32, (WIDE, STATE), 0) // HEAD + group * GROUP
    ones = (place == lax.broadcasted_iota(jnp.int32, (WIDE, STATE), 1)).astype(bf16)
    dtotal[...] += split_dot(wide(total_parts), ones)
    dstep[...] += split_dot(wide(step_parts), ones)
    dmixed = wide(dx_parts) * silu_slope(mixed, gate)
    dvalues, rows = convolve_back(dmixed, values, taps_ref[0:4], near)
    dproj_ref[:, pl.ds(pl.multiple_of(group * WIDE, WIDE), WIDE)] = dvalues.astype(bf16)
    drows_ref[0, :, pl.ds(pl.multiple_of(group * WIDE, WIDE), WIDE)] = jnp.concatenate(
        rows + [wide(skip_parts), jnp.zeros((2, WIDE), f32)], axis=0
    )

    @pl.when(group == last)
    def _():
        shared = shared_ref[...]
        values = shared[:, : 2 * STATE]
        mixed = convolve(values, taps_shared_ref[0:4], taps_shared_ref[4:5], near)
        gate = sigmoid(mixed)
        low = dscores[...].astype(bf16)
        db = jnp.dot(low, c_keep[...], preferred_element_type=f32)
        dc = lax.dot_general(
            low, b_keep[...], (((0,), (0,)), ((), ())), preferred_element_type=f32
        )
        dmixed = jnp.concatenate([db, dc], axis=1) * silu_slope(mixed, gate)
        dvalues, rows = convolve_back(dmixed, values, taps_shared_ref[0:4], near)
        at = dproj_ref.shape[1] - 3 * STATE
        drows_ref[0, :, at : at + 2 * STATE] = jnp.concatenate(
            rows + [jnp.zeros((3, 2 * STATE), f32)], axis=0
        )
        raw, step, rate, total = steps_of(shared[:, 2 * STATE :], head_ref[...])
        row, col = positions()
        upper = (row <= col).astype(f32)
        drate = jnp.dot(upper, dtotal[...], precision=highest, preferred_element_type=f32)
        draw = (dstep[...] - drate * head_ref[1:2]) * sigmoid(raw)
        dproj_ref[:, at : at + 2 * STATE] = dvalues.astype(bf16)
        dproj_ref[:, at + 2 * STATE :] = draw.astype(bf16)
        drows_ref[0, :, at + 2 * STATE :] = jnp.concatenate(
            [
                jnp.sum(draw, axis=0, keepdims=True),
                jnp.sum(drate * rate, axis=0, keepdims=True),
                jnp.zeros((6, STATE), f32),
            ],
            axis=0,
        )


def mixer_specs(columns):
    return [
        pl.BlockSpec((LEN, WIDE), lambda s, g: (s, g)),
        pl.BlockSpec((LEN, 3 * STATE), lambda s, g: (s, columns // (3 * STATE))),
        pl.BlockSpec((LEN, 8), lambda s, g: (s, 0)),
        pl.BlockSpec((LEN, 1), lambda s, g: (s, 0)),
        pl.BlockSpec((1, 1, LEN), lambda s, g: (s, 0, 0)),
        pl.BlockSpec((8, WIDE), lambda s, g: (0, g)),
        pl.BlockSpec((8, 2 * STATE), lambda s, g: (0, 0)),
        pl.BlockSpec((8, STATE), lambda s, g: (0, 0)),
    ]


def mixer_scratch(groups):
    return [
        pltpu.VMEM((LEN, LEN), f32),
        pltpu.VMEM((LEN, LEN), f32),
        pltpu.VMEM((groups, LEN, STATE), f32),
        pltpu.VMEM((STATE, LEN), f32),
        pltpu.VMEM((groups, LEN, STATE), f32),
    ]


def mix_forward(proj, near, seg_col, seg_row, taps, taps_shared, heads):
    rows, columns = proj.shape[0], proj.shape[1] - 3 * STATE
    groups = columns // WIDE
    return pl.pallas_call(
        mix_forward_kernel,
        grid=(rows // LEN, groups),
        in_specs=mixer_specs(columns),
        out_specs=pl.BlockSpec((LEN, WIDE), lambda s, g: (s, g)),
        out_shape=jax.ShapeDtypeStruct((rows, columns), f32),
        scratch_shapes=mixer_scratch(groups),
        compiler_params=pltpu.CompilerParams(vmem_limit_bytes=VMEM),
        cost_estimate=pl.CostEstimate(flops=10**9, bytes_accessed=8 * 2**20, transcendentals=10**7),
        name="mix_forward",
    )(proj, proj, near, seg_col, seg_row, taps, taps_shared, heads)


def mix_backward(proj, near, seg_col, seg_row, taps, taps_shared, heads, ssd, dssd):
    rows, columns = proj.shape[0], proj.shape[1] - 3 * STATE
    groups, seqs = columns // WIDE, rows // LEN
    wide = pl.BlockSpec((LEN, WIDE), lambda s, g: (s, g))
    return pl.pallas_call(
        mix_backward_kernel,
        grid=(seqs, groups),
        in_specs=mixer_specs(columns) + [wide, wide],
        out_specs=[
            pl.BlockSpec((LEN, columns + 3 * STATE), lambda s, g: (s, 0)),
            pl.BlockSpec((1, 8, columns + 3 * STATE), lambda s, g: (s, 0, 0)),
        ],
        out_shape=[
            jax.ShapeDtypeStruct(proj.shape, bf16),
            jax.ShapeDtypeStruct((seqs, 8, proj.shape[1]), f32),
        ],
        scratch_shapes=mixer_scratch(groups)
        + [
            pltpu.VMEM((LEN, STATE), bf16),
            pltpu.VMEM((LEN, STATE), bf16),
            pltpu.VMEM((LEN, LEN), f32),
            pltpu.VMEM((LEN, STATE), f32),
            pltpu.VMEM((LEN, STATE), f32),
        ],
        compiler_params=pltpu.CompilerParams(vmem_limit_bytes=VMEM),
        cost_estimate=pl.CostEstimate(flops=3 * 10**9, bytes_accessed=12 * 2**20, transcendentals=10**7),
        name="mix_backward",
    )(proj, proj, near, seg_col, seg_row, taps, taps_shared, heads, ssd, dssd)


SMALL = 8


def two_parts(rows):
    high = rows.astype(bf16).astype(f32)
    return [high, rows - high]


OVER_TOKENS = (((0,), (0,)), ((), ()))


def grad_pieces_kernel(left_ref, right_ref, small_ref, extra_ref, *out_refs):
    rows = left_ref.shape[1] // SIDE
    small = jnp.concatenate(two_parts(small_ref[0] + small_ref[1] + extra_ref[...]), axis=0)
    for k, out_ref in enumerate(out_refs):
        out_ref[:rows] = lax.dot_general(
            left_ref[:, k * rows : (k + 1) * rows], right_ref[...], OVER_TOKENS,
            preferred_element_type=f32,
        ).astype(out_ref.dtype)
        out_ref[rows:] = small.astype(out_ref.dtype)


def grad_pieces(left, right, small, extra):
    rows, columns = left.shape[1] // SIDE + 2 * SMALL, right.shape[1]
    wide = columns // 3
    return pl.pallas_call(
        grad_pieces_kernel,
        grid=(3,),
        in_specs=[
            pl.BlockSpec(left.shape, lambda j: (0, 0)),
            pl.BlockSpec((right.shape[0], wide), lambda j: (0, j)),
            pl.BlockSpec((2, SMALL, wide), lambda j: (0, 0, j)),
            pl.BlockSpec((SMALL, wide), lambda j: (0, j)),
        ],
        out_specs=[pl.BlockSpec((rows, wide), lambda j: (0, j))] * SIDE,
        out_shape=[
            jax.ShapeDtypeStruct((rows, columns), bf16 if k else f32) for k in range(SIDE)
        ],
        compiler_params=pltpu.CompilerParams(vmem_limit_bytes=VMEM),
        cost_estimate=pl.CostEstimate(
            flops=2 * SIDE * rows * columns * left.shape[0], bytes_accessed=10 * 2**20, transcendentals=0
        ),
        name="grad_pieces",
    )(left, right, small, extra)


def tokens_kernel(
    core_ref, dgate_ref, gate_ref, dproj_ref, reorder_ref, own_mixed_ref, other_mixed_ref, out_ref,
    *refs,
):
    mix_refs = refs[:SIDE]
    own_ref, other_ref, branch_own_ref, branch_other_ref, total, branch = refs[SIDE:]
    step = pl.program_id(0)
    core = core_ref[0]
    turned = (((1,), (1,)), ((), ()))
    wide = gate_ref.shape[0]
    for k, ref in enumerate(mix_refs):

        @pl.when(step == k)
        def _(k=k, ref=ref):
            back = lax.dot_general(dproj_ref[...], ref[...], turned, preferred_element_type=f32)
            back = lax.dot_general(
                back.astype(bf16), reorder_ref[...], turned, preferred_element_type=f32
            )
            if k == 0:
                total[...] = back
            else:
                total[...] += back

    at = pl.ds(pl.multiple_of(step * wide, wide), wide)
    total[:, at] += lax.dot_general(dgate_ref[...], gate_ref[...], turned, preferred_element_type=f32)
    mixed = jnp.where(step // (SIDE // 2) == core, own_mixed_ref[...], other_mixed_ref[...])
    part = jnp.dot(mixed, out_ref[...], preferred_element_type=f32)

    @pl.when(step == 0)
    def _():
        branch[...] = part

    @pl.when(step > 0)
    def _():
        branch[...] += part

    @pl.when(step == SIDE - 1)
    def _():
        own = pl.ds(pl.multiple_of(core * LEN, LEN), LEN)
        other = pl.ds(pl.multiple_of((1 - core) * LEN, LEN), LEN)
        own_ref[...] = total[own, :]
        other_ref[...] = total[other, :].astype(bf16)
        branch_own_ref[...] = branch[own, :].astype(bf16)
        branch_other_ref[...] = branch[other, :].astype(bf16)


def tokens_parts(core, dgate, w_rest, dproj, reorder, own_mixed, other_mixed, w_out, w_mix):
    rows, width, half = dproj.shape[0], reorder.shape[0], own_mixed.shape[1]
    wide = width // SIDE
    full = lambda array: pl.BlockSpec(array.shape, lambda j: (0, 0))
    mixed = pl.BlockSpec((rows, 2 * half // SIDE), lambda j: (0, j % (SIDE // 2)))
    return pl.pallas_call(
        tokens_kernel,
        grid=(SIDE,),
        in_specs=[
            pl.BlockSpec(memory_space=pltpu.SMEM),
            full(dgate),
            pl.BlockSpec((wide, dgate.shape[1]), lambda j: (j, 0)),
            full(dproj),
            pl.BlockSpec((width, wide), lambda j: (0, j)),
            mixed,
            mixed,
            pl.BlockSpec((2 * half // SIDE, w_out.shape[1]), lambda j: (j, 0)),
        ]
        + [full(piece) for piece in w_mix],
        out_specs=[pl.BlockSpec((LEN, width), lambda j: (0, 0))] * 2
        + [pl.BlockSpec((LEN, w_out.shape[1]), lambda j: (0, 0))] * 2,
        out_shape=[
            jax.ShapeDtypeStruct((LEN, width), f32),
            jax.ShapeDtypeStruct((LEN, width), bf16),
        ]
        + [jax.ShapeDtypeStruct((LEN, w_out.shape[1]), bf16)] * 2,
        scratch_shapes=[pltpu.VMEM((rows, width), f32), pltpu.VMEM((rows, w_out.shape[1]), f32)],
        compiler_params=pltpu.CompilerParams(vmem_limit_bytes=56 * 2**20),
        cost_estimate=pl.CostEstimate(
            flops=10**10, bytes_accessed=32 * 2**20, transcendentals=0
        ),
        name="tokens_parts",
    )(core, dgate, w_rest, dproj, reorder, own_mixed, other_mixed, w_out, *w_mix)


def fold_kernel(own_ref, one_ref, two_ref, three_ref, extra_ref, out_ref, *send_refs):
    rows = own_ref.shape[0] // 16 * 16
    kept = (own_ref.shape[0] - 2 * SMALL) // 16 * 16
    refs = (own_ref, one_ref, two_ref, three_ref)
    part = kept // 4
    small = extra_ref[...]
    for ref in refs:
        tail = ref[kept : kept + 2 * SMALL].astype(f32)
        small = small + tail[:SMALL] + tail[SMALL:]
    fill = [jnp.zeros((out_ref.shape[0] - part - 2 * SMALL, small.shape[1]), f32)]
    fill = fill if fill[0].shape[0] else []
    for k in range(4):
        total = sum(ref[k * part : (k + 1) * part].astype(f32) for ref in refs)
        if k == 0:
            out_ref[...] = jnp.concatenate([total, small, jnp.zeros_like(small)] + fill, axis=0)
        else:
            send_refs[k - 1][...] = jnp.concatenate(
                [total] + two_parts(small) + fill, axis=0
            ).astype(bf16)


def fold(own, received, extra):
    columns = own.shape[1]
    kept = (own.shape[0] - 2 * SMALL) // 16 * 16
    rows = -(-(kept // 4 + 2 * SMALL) // 16) * 16
    wide = columns // 5
    block = pl.BlockSpec((own.shape[0], wide), lambda j: (0, j))
    out = pl.BlockSpec((rows, wide), lambda j: (0, j))
    return pl.pallas_call(
        fold_kernel,
        grid=(5,),
        in_specs=[block] * 4 + [pl.BlockSpec((SMALL, wide), lambda j: (0, j))],
        out_specs=[out] * 4,
        out_shape=[jax.ShapeDtypeStruct((rows, columns), f32)]
        + [jax.ShapeDtypeStruct((rows, columns), bf16)] * 3,
        compiler_params=pltpu.CompilerParams(vmem_limit_bytes=VMEM),
        cost_estimate=pl.CostEstimate(flops=10**7, bytes_accessed=8 * 2**20, transcendentals=0),
        name="fold",
    )(own, *received, extra)


def owners_kernel(core_ref, own_ref, other_ref, cot_ref, normed_ref, dgate_ref, out_ref):
    shards, width = out_ref.shape[0], out_ref.shape[2]
    mine = pl.program_id(0) // (pl.num_programs(0) // 2) == core_ref[0]
    mixed = jnp.where(mine, own_ref[...], other_ref[...])
    grad_out = lax.dot_general(
        mixed, cot_ref[...], OVER_TOKENS, preferred_element_type=f32
    ).reshape(shards, -1, width)
    grad_gate = lax.dot_general(
        normed_ref[...], dgate_ref[...], OVER_TOKENS, preferred_element_type=f32
    )
    grad_gate = grad_gate.reshape(shards, -1, 2 * width)
    out_ref[...] = jnp.concatenate(
        [grad_out, grad_gate[:, :, :width], grad_gate[:, :, width:]], axis=1
    ).astype(bf16)


def owners_grads(core, own, other, cot, normed, dgate, shards):
    steps = 4
    each = shards // steps
    width = cot.shape[1]
    rows_out, rows_in = 2 * own.shape[1] // shards, normed.shape[1] // shards
    mixed = pl.BlockSpec((own.shape[0], each * rows_out), lambda j: (0, j % (steps // 2)))
    rows = rows_out + 2 * rows_in
    return pl.pallas_call(
        owners_kernel,
        grid=(steps,),
        in_specs=[
            pl.BlockSpec(memory_space=pltpu.SMEM),
            mixed,
            mixed,
            pl.BlockSpec(cot.shape, lambda j: (0, 0)),
            pl.BlockSpec((normed.shape[0], each * rows_in), lambda j: (0, j)),
            pl.BlockSpec(dgate.shape, lambda j: (0, 0)),
        ],
        out_specs=pl.BlockSpec((each, rows, width), lambda j: (j, 0, 0)),
        out_shape=jax.ShapeDtypeStruct((shards, rows, width), bf16),
        compiler_params=pltpu.CompilerParams(vmem_limit_bytes=VMEM),
        cost_estimate=pl.CostEstimate(
            flops=2 * cot.shape[0] * shards * rows * width, bytes_accessed=16 * 2**20, transcendentals=0
        ),
        name="owners_grads",
    )(core, own, other, cot, normed, dgate)


CHIPS = ("z", "y", "x")
ALL = ("grp",) + CHIPS
SIDE = 4
ORDERS = (("x", "y", "z"), ("y", "z", "x"))


def place(core, spot):
    index = core
    for axis in CHIPS:
        index = index * SIDE + spot[axis] % SIDE
    return index


def moved(value, phase, by, orders=ORDERS):
    pairs = []
    for core in range(2):
        for z in range(SIDE):
            for y in range(SIDE):
                for x in range(SIDE):
                    spot = dict(z=z, y=y, x=x)
                    axis = orders[core][phase]
                    pairs.append((place(core, spot), place(core, {**spot, axis: spot[axis] + by})))
    return lax.ppermute(value, ALL, pairs)


def swapped(value):
    return lax.ppermute(value, "grp", [(0, 1), (1, 0)])


def in_order(own, other, axis=0):
    first = lax.axis_index("grp") == 0
    return jnp.concatenate([jnp.where(first, own, other), jnp.where(first, other, own)], axis=axis)


def turned(value, dim, by):
    twice = jnp.concatenate([value, value], axis=dim)
    return lax.dynamic_slice_in_dim(twice, by, value.shape[dim], dim)


def gathered(own, orders):
    for phase in (2, 1):
        own = jnp.concatenate([own] + [moved(own, phase, -k, orders) for k in range(1, SIDE)])
    return [own] + [moved(own, 0, -k, orders) for k in range(1, SIDE)]


def row_places(rows, orders):
    index = lax.iota(jnp.int32, SIDE**3 * rows)
    steps = (index // (SIDE * SIDE * rows), index // (SIDE * rows) % SIDE, index // rows % SIDE)
    core = lax.axis_index("grp")
    places = []
    for order in orders:
        spot = {axis: (lax.axis_index(axis) + step) % SIDE for axis, step in zip(order, steps)}
        places.append(((spot["z"] * SIDE + spot["y"]) * SIDE + spot["x"]) * rows + index % rows)
    return jnp.where(core == 0, places[0], places[1])


def halved(array, size, dim, other=False):
    core = lax.axis_index("grp")
    return lax.dynamic_slice_in_dim(array, (1 - core if other else core) * size, size, dim)


def times(left, right):
    return jnp.dot(left, right, preferred_element_type=f32)


def times_turned(left, right):
    return lax.dot_general(left, right, (((1,), (1,)), ((), ())), preferred_element_type=f32)


def on_device(
    tokens,
    segment_ids,
    norm_gain,
    in_weight,
    conv_weight,
    conv_bias,
    dt_bias,
    a_log,
    skip_d,
    gnorm_gain,
    out_weight,
    cotangent,
):
    width = tokens.shape[1]
    inner = gnorm_gain.shape[0]
    half = inner // 2
    heads = dt_bias.shape[0] // 2
    bc = conv_bias.shape[0] - inner
    rows_in, rows_out = in_weight.shape[0], out_weight.shape[0]
    shards = SIDE**3

    own_mix = jnp.concatenate(
        [
            halved(in_weight[:, inner : 2 * inner], half, 1),
            in_weight[:, 2 * inner : 2 * inner + bc],
            halved(in_weight[:, inner + inner + bc :], heads, 1),
            jnp.zeros((rows_in, STATE - heads), bf16),
        ],
        axis=1,
    )
    own_out = halved(out_weight, width // 2, 1)
    own_rest = jnp.concatenate(
        [halved(in_weight[:, :inner], half, 1), own_out[:rows_in], own_out[rows_in:]], axis=1
    )
    w_rest = lax.all_gather(own_rest, CHIPS, axis=0, tiled=True)
    w_mix = gathered(own_mix, ORDERS)

    residual = tokens.astype(f32)
    scale = lax.rsqrt(jnp.mean(residual * residual, axis=-1, keepdims=True) + NORM_EPS)
    unit = residual * scale
    own_low = (unit * norm_gain).astype(bf16)
    normed = in_order(own_low, swapped(own_low))
    cot = in_order(cotangent, swapped(cotangent))
    segments = in_order(segment_ids, swapped(segment_ids))
    near = [jnp.zeros(segments.shape, f32)]
    for back in range(1, TAPS):
        same = (segments[:, back:] == segments[:, :-back]).astype(f32)
        near.append(jnp.pad(same, ((0, 0), (back, 0))))
    near = jnp.stack(near + [near[0]] * 4, axis=-1).reshape(-1, 8)
    seg_col = segments.astype(f32).reshape(-1, 1)
    seg_row = segments.astype(f32)[:, None, :]

    taps = jnp.concatenate(
        [
            halved(conv_weight[:, :inner], half, 1),
            halved(conv_bias[None, :inner], half, 1),
            jnp.repeat(halved(skip_d, heads, 0), HEAD)[None],
            halved(gnorm_gain[None], half, 1),
            jnp.zeros((1, half), f32),
        ]
    )
    taps_shared = jnp.concatenate(
        [conv_weight[:, inner:], conv_bias[None, inner:], jnp.zeros((3, bc), f32)]
    )
    head_rows = jnp.stack([halved(dt_bias, heads, 0), jnp.exp(halved(a_log, heads, 0))])
    head_rows = jnp.pad(head_rows, ((0, 6), (0, STATE - heads)))
    gain = halved(gnorm_gain, half, 0)

    places = row_places(rows_in, ORDERS)
    reorder = (lax.iota(jnp.int32, width)[:, None] == places[None, :]).astype(bf16)
    normed_moved = times(normed, reorder).astype(bf16)
    cot_half = halved(cot, width // 2, 1)

    core = lax.axis_index("grp")
    which = core.astype(jnp.int32)[None]
    quarter = width // SIDE
    proj = sum(
        times(normed_moved[:, k * quarter : (k + 1) * quarter], w_mix[k]) for k in range(SIDE)
    )
    sides = (near, seg_col, seg_row, taps, taps_shared, head_rows)
    ssd = mix_forward(proj, *sides)
    ssd, w_rest, reorder, cot_half, normed = lax.optimization_barrier(
        (ssd, w_rest, reorder, cot_half, normed)
    )
    w_out = jnp.stack(
        [
            w_rest[:, half : half + width // 2].reshape(shards, rows_in, -1),
            w_rest[:, half + width // 2 :].reshape(shards, rows_in, -1),
        ],
        axis=1,
    ).reshape(inner, -1)
    mixer_parts = times_turned(cot_half, w_out).astype(bf16)
    grad_mixer = halved(mixer_parts, half, 1).astype(f32) + swapped(
        halved(mixer_parts, half, 1, other=True)
    ).astype(f32)
    gate_part = times(normed, w_rest[:, :half])
    opened = sigmoid(gate_part)
    gate = gate_part * opened
    gated = ssd * gate
    weighted = grad_mixer * gain
    sums = jnp.stack([jnp.sum(gated * gated, axis=-1), jnp.sum(gated * weighted, axis=-1)])
    sums = sums + swapped(sums)
    gscale = lax.rsqrt(sums[0] / inner + NORM_EPS)[:, None]
    pull = gscale * gscale * gscale * (sums[1] / inner)[:, None]
    dgated = gscale * weighted - gated * pull
    mixer_low = (gated * gscale * gain).astype(bf16)
    grad_gain = jnp.sum(grad_mixer * gated * gscale, axis=0)
    dgate_low = (dgated * ssd * silu_slope(gate_part, opened)).astype(bf16)
    dssd = (dgated * gate).astype(bf16)
    mixer_other = swapped(mixer_low)

    rest_grad = owners_grads(which, mixer_low, mixer_other, cot_half, normed, dgate_low, shards)
    rest_rows = rest_grad.shape[1]
    gain_row = jnp.zeros((SMALL, proj.shape[1]), f32).at[6, :half].set(grad_gain)
    rest_grad, dssd, gain_row = lax.optimization_barrier((rest_grad, dssd, gain_row))
    rest_share = lax.psum_scatter(
        rest_grad.reshape(shards * rest_rows, -1), ("z", "y"), scatter_dimension=0, tiled=True
    )

    dproj, drows = mix_backward(proj, *sides, ssd, dssd)
    own, *gone = grad_pieces(normed_moved, dproj, drows, gain_row)
    dproj, *gone = lax.optimization_barrier((dproj, *gone))
    received = [moved(gone[k - 1], 0, k) for k in range(1, SIDE)]

    parts = tokens_parts(
        which, dgate_low, w_rest, dproj, reorder, mixer_low, mixer_other, w_out, w_mix
    )
    nothing = jnp.zeros((SMALL, dproj.shape[1]), f32)
    *received, nothing, parts = lax.optimization_barrier((*received, nothing, parts))
    own, *gone = fold(own, received, nothing)
    parts, *gone = lax.optimization_barrier((parts, *gone))
    received = [moved(gone[k - 1], 1, k) for k in range(1, SIDE)]
    normed_own, normed_other, branch_own, branch_other = parts
    branch = in_order(branch_own, swapped(branch_other), axis=1)
    out_tokens = (residual + branch.astype(f32)).astype(bf16)
    grad_normed = normed_own + swapped(normed_other).astype(f32)
    q = grad_normed * norm_gain
    grad_tokens = cotangent.astype(f32) + scale * (
        q - unit * jnp.mean(q * unit, axis=-1, keepdims=True)
    )
    grad_norm_gain = jnp.sum(grad_normed * unit, axis=0)[None]
    for phase in range(2):
        grad_norm_gain = grad_norm_gain + sum(
            moved(grad_norm_gain, phase, k) for k in range(1, SIDE)
        )
    extra = nothing.at[SMALL - 1, :width].set(grad_norm_gain[0])
    own, *gone = fold(own, received, extra)

    rest_turned = turned(rest_share.reshape(SIDE, rest_rows, -1), 0, lax.axis_index("x"))
    rest_turned, *gone = lax.optimization_barrier((rest_turned, *gone))
    mix_total = own + sum(moved(gone[k - 1], 2, k).astype(f32) for k in range(1, SIDE))
    mix_share = mix_total[:rows_in]
    small = mix_total[rows_in : rows_in + SMALL] + mix_total[rows_in + SMALL : rows_in + 2 * SMALL]
    rest_total = rest_turned[0].astype(f32) + sum(
        lax.ppermute(rest_turned[k], "x", [(i, (i + k) % SIDE) for i in range(SIDE)]).astype(f32)
        for k in range(1, SIDE)
    )

    small_other = swapped(small)
    mix_other, rest_other = swapped(mix_share), swapped(rest_total)
    bc_sum = (mix_share + mix_other)[:, half : half + bc]
    dt_at = slice(half + bc, half + bc + heads)
    gate_total, gate_other = (
        jnp.concatenate([rest[rows_out : rows_out + rows_in], rest[rows_out + rows_in :]], axis=1)
        for rest in (rest_total, rest_other)
    )
    grad_in_weight = jnp.concatenate(
        [
            in_order(gate_total, gate_other, axis=1),
            in_order(mix_share[:, :half], mix_other[:, :half], axis=1),
            bc_sum,
            in_order(mix_share[:, dt_at], mix_other[:, dt_at], axis=1),
        ],
        axis=1,
    )
    grad_out_weight = in_order(rest_total[:rows_out], rest_other[:rows_out], axis=1)
    both = in_order(small[:, :half], small_other[:, :half], axis=1)
    summed = small + small_other
    shared_rows = summed[:, half : half + bc]
    head_sums = in_order(small[:, dt_at], small_other[:, dt_at], axis=1)
    return (
        out_tokens,
        grad_tokens,
        summed[SMALL - 1, :width],
        grad_in_weight,
        jnp.concatenate([both[:4], shared_rows[:4]], axis=1),
        jnp.concatenate([both[4], shared_rows[4]]),
        head_sums[0],
        head_sums[1],
        both[5].reshape(-1, HEAD).sum(axis=-1),
        both[6],
        grad_out_weight,
    )


def solution(mesh):
    chips = Mesh(mesh.devices.reshape(2, SIDE, SIDE, SIDE), ALL)
    rows = P(ALL, None)
    owned = P(CHIPS, None)
    return jax.shard_map(
        on_device,
        mesh=chips,
        in_specs=(rows, rows, P(), owned, P(), P(), P(), P(), P(), P(), owned, rows),
        out_specs=(rows, rows, P(), owned, P(), P(), P(), P(), P(), P(), owned),
        check_vma=False,
    )
```

```python
import functools

import jax
import jax.numpy as jnp
import numpy as np
from jax import lax
from jax.experimental import pallas as pl
from jax.experimental.pallas import tpu as pltpu
from jax.sharding import Mesh
from jax.sharding import PartitionSpec as P

LEN = 256
VMEM = 24 * 2**20
HALF = 128
HEAD = 64
GROUP = 8
WIDE = GROUP * HEAD
STATE = 128
TAPS = 4
NORM_EPS = 1e-05
LOG2E = 1.4426950408889634
FAR = -1e30
bf16 = jnp.bfloat16
f32 = jnp.float32
highest = lax.Precision.HIGHEST


def sigmoid(v):
    return 0.5 + 0.5 * jnp.tanh(0.5 * v)


def convolve(values, taps, bias, near):
    total = bias + taps[TAPS - 1 : TAPS] * values
    for back in range(1, TAPS):
        tap = taps[TAPS - 1 - back : TAPS - back]
        total = total + tap * (near[:, back : back + 1] * pltpu.roll(values, back, 0))
    return total


def convolve_back(grad, values, taps, near):
    total = taps[TAPS - 1 : TAPS] * grad
    rows = [jnp.sum(grad * values, axis=0, keepdims=True)]
    for back in range(1, TAPS):
        tap = taps[TAPS - 1 - back : TAPS - back]
        seen = pltpu.roll(near[:, back : back + 1] * grad, LEN - back, 0)
        total = total + tap * seen
        rows.append(jnp.sum(seen * values, axis=0, keepdims=True))
    return total, rows[::-1] + [jnp.sum(grad, axis=0, keepdims=True)]


def silu_slope(v, s):
    return s * (1.0 + v * (1.0 - s))


def positions():
    return (
        lax.broadcasted_iota(jnp.int32, (LEN, LEN), 0),
        lax.broadcasted_iota(jnp.int32, (LEN, LEN), 1),
    )


def softplus(v):
    small = jnp.exp(-jnp.abs(v))
    return jnp.maximum(v, 0.0) + jnp.log1p(small)


def steps_of(dt_part, head_rows):
    raw = dt_part + head_rows[0:1]
    step = softplus(raw)
    rate = -step * head_rows[1:2]
    row, col = positions()
    lower = (row >= col).astype(f32)
    total = jnp.dot(lower, rate, precision=highest, preferred_element_type=f32) * LOG2E
    return raw, step, rate, total


def split_dot(values, ones):
    high = values.astype(bf16)
    low = (values - high.astype(f32)).astype(bf16)
    return jnp.dot(high, ones, preferred_element_type=f32) + jnp.dot(
        low, ones, preferred_element_type=f32
    )


def pair_columns(table, pair):
    lane = lax.broadcasted_iota(jnp.int32, (LEN, 2 * HEAD), 1)
    return jnp.where(lane < HEAD, table[:, 2 * pair : 2 * pair + 1], table[:, 2 * pair + 1 : 2 * pair + 2])


def halves(values):
    lane = lax.broadcasted_iota(jnp.int32, values.shape, 1)
    zero = jnp.zeros_like(values)
    return jnp.where(lane < HEAD, values, zero), jnp.where(lane >= HEAD, values, zero)


def mix_forward_kernel(
    proj_ref, shared_ref, near_ref, seg_col_ref, seg_row_ref, taps_ref, taps_shared_ref, head_ref,
    ssd_ref, scores, apart, totals, totals_row, steps,
):
    group = pl.program_id(1)
    near = near_ref[...]

    @pl.when(group == 0)
    def _():
        shared = shared_ref[...]
        mixed = convolve(shared[:, : 2 * STATE], taps_shared_ref[0:4], taps_shared_ref[4:5], near)
        mixed = mixed * sigmoid(mixed)
        b_low = mixed[:, :STATE].astype(bf16)
        c_low = mixed[:, STATE:].astype(bf16)
        scores[...] = lax.dot_general(
            c_low, b_low, (((1,), (1,)), ((), ())), preferred_element_type=f32
        )
        row, col = positions()
        seen = (row >= col) & (seg_col_ref[...] == seg_row_ref[0])
        apart[...] = jnp.where(seen, 0.0, FAR)
        raw, step, rate, total = steps_of(shared[:, 2 * STATE :], head_ref[...])
        for g in range(totals.shape[0]):
            turn = (STATE - GROUP * g) % STATE
            totals[g] = pltpu.roll(total, turn, 1) if turn else total
            steps[g] = pltpu.roll(step, turn, 1) if turn else step
        totals_row[...] = total.T

    values = proj_ref[...]
    mixed = convolve(values, taps_ref[0:4], taps_ref[4:5], near)
    x = mixed * sigmoid(mixed)
    total = totals[group]
    step = steps[group]
    total_row = totals_row[pl.ds(pl.multiple_of(group * GROUP, GROUP), GROUP), :]
    skip = taps_ref[5:6]
    for pair in range(GROUP // 2):
        lanes = slice(2 * HEAD * pair, 2 * HEAD * (pair + 1))
        x_pair = x[:, lanes]
        sides = halves((pair_columns(step, pair) * x_pair).astype(bf16))
        upper = lower = 0.0
        for side in range(2):
            head = 2 * pair + side
            col = total[:, head : head + 1]
            row = total_row[head : head + 1, :]
            decay = jnp.exp2(col[:HALF] - row[:, :HALF] + apart[:HALF, :HALF])
            weight = (scores[:HALF, :HALF] * decay).astype(bf16)
            upper = upper + jnp.dot(weight, sides[side][:HALF], preferred_element_type=f32)
            decay = jnp.exp2(col[HALF:] - row + apart[HALF:, :])
            weight = (scores[HALF:, :] * decay).astype(bf16)
            lower = lower + jnp.dot(weight, sides[side], preferred_element_type=f32)
        skipped = skip[:, lanes] * x_pair
        ssd_ref[:HALF, lanes] = upper + skipped[:HALF]
        ssd_ref[HALF:, lanes] = lower + skipped[HALF:]


def mix_backward_kernel(
    proj_ref, shared_ref, near_ref, seg_col_ref, seg_row_ref, taps_ref, taps_shared_ref, head_ref,
    ssd_ref, dssd_ref,
    dproj_ref, drows_ref,
    scores, apart, totals, totals_row, steps, b_keep, c_keep, dscores, dtotal, dstep,
):
    group = pl.program_id(1)
    last = pl.num_programs(1) - 1
    near = near_ref[...]

    @pl.when(group == 0)
    def _():
        shared = shared_ref[...]
        mixed = convolve(shared[:, : 2 * STATE], taps_shared_ref[0:4], taps_shared_ref[4:5], near)
        mixed = mixed * sigmoid(mixed)
        b_low = mixed[:, :STATE].astype(bf16)
        c_low = mixed[:, STATE:].astype(bf16)
        b_keep[...] = b_low
        c_keep[...] = c_low
        scores[...] = lax.dot_general(
            b_low, c_low, (((1,), (1,)), ((), ())), preferred_element_type=f32
        )
        row, col = positions()
        seen = (row <= col) & (seg_col_ref[...] == seg_row_ref[0])
        apart[...] = jnp.where(seen, 0.0, FAR)
        raw, step, rate, total = steps_of(shared[:, 2 * STATE :], head_ref[...])
        for g in range(totals.shape[0]):
            turn = (STATE - GROUP * g) % STATE
            totals[g] = pltpu.roll(total, turn, 1) if turn else total
            steps[g] = pltpu.roll(step, turn, 1) if turn else step
        totals_row[...] = total.T
        dscores[...] = jnp.zeros_like(dscores)
        dtotal[...] = jnp.zeros_like(dtotal)
        dstep[...] = jnp.zeros_like(dstep)

    values = proj_ref[...]
    mixed = convolve(values, taps_ref[0:4], taps_ref[4:5], near)
    gate = sigmoid(mixed)
    x = mixed * gate
    total = totals[group]
    step = steps[group]
    total_row = totals_row[pl.ds(pl.multiple_of(group * GROUP, GROUP), GROUP), :]
    skip = taps_ref[5:6]
    dx_parts, total_parts, step_parts, skip_parts = [], [], [], []
    for pair in range(GROUP // 2):
        lanes = slice(2 * HEAD * pair, 2 * HEAD * (pair + 1))
        x_pair = x[:, lanes]
        dt_pair = pair_columns(step, pair)
        low_x = (dt_pair * x_pair).astype(bf16)
        low_dy = dssd_ref[:, lanes]
        dy = low_dy.astype(f32)
        x_sides = halves(low_x)
        dy_sides = halves(low_dy)
        upper = lower = upper_scores = lower_scores = 0.0
        for side in range(2):
            head = 2 * pair + side
            col = total[:, head : head + 1]
            row = total_row[head : head + 1, :]
            decay = jnp.exp2(row - col[:HALF] + apart[:HALF, :])
            weight = (scores[:HALF, :] * decay).astype(bf16)
            upper = upper + jnp.dot(weight, dy_sides[side], preferred_element_type=f32)
            grad = lax.dot_general(
                x_sides[side][:HALF], low_dy, (((1,), (1,)), ((), ())), preferred_element_type=f32
            )
            upper_scores = upper_scores + grad * decay
            decay = jnp.exp2(row[:, HALF:] - col[HALF:] + apart[HALF:, HALF:])
            weight = (scores[HALF:, HALF:] * decay).astype(bf16)
            lower = lower + jnp.dot(weight, dy_sides[side][HALF:], preferred_element_type=f32)
            grad = lax.dot_general(
                x_sides[side][HALF:], low_dy[HALF:], (((1,), (1,)), ((), ())),
                preferred_element_type=f32,
            )
            lower_scores = lower_scores + grad * decay
        dscores[:HALF, :] += upper_scores
        dscores[HALF:, HALF:] += lower_scores
        back = jnp.concatenate([upper, lower], axis=0)
        skip_pair = skip[:, lanes]
        inside = ssd_ref[:, lanes] - skip_pair * x_pair
        total_parts.append(dy * inside - low_x.astype(f32) * back)
        step_parts.append(x_pair * back)
        skip_parts.append(jnp.sum(dy * x_pair, axis=0, keepdims=True))
        dx_parts.append(dt_pair * back + skip_pair * dy)
    wide = lambda parts: jnp.concatenate(parts, axis=1)
    place = lax.broadcasted_iota(jnp.int32, (WIDE, STATE), 0) // HEAD + group * GROUP
    ones = (place == lax.broadcasted_iota(jnp.int32, (WIDE, STATE), 1)).astype(bf16)
    dtotal[...] += split_dot(wide(total_parts), ones)
    dstep[...] += split_dot(wide(step_parts), ones)
    dmixed = wide(dx_parts) * silu_slope(mixed, gate)
    dvalues, rows = convolve_back(dmixed, values, taps_ref[0:4], near)
    dproj_ref[:, pl.ds(pl.multiple_of(group * WIDE, WIDE), WIDE)] = dvalues.astype(bf16)
    drows_ref[0, :, pl.ds(pl.multiple_of(group * WIDE, WIDE), WIDE)] = jnp.concatenate(
        rows + [wide(skip_parts), jnp.zeros((2, WIDE), f32)], axis=0
    )

    @pl.when(group == last)
    def _():
        shared = shared_ref[...]
        values = shared[:, : 2 * STATE]
        mixed = convolve(values, taps_shared_ref[0:4], taps_shared_ref[4:5], near)
        gate = sigmoid(mixed)
        low = dscores[...].astype(bf16)
        db = jnp.dot(low, c_keep[...], preferred_element_type=f32)
        dc = lax.dot_general(
            low, b_keep[...], (((0,), (0,)), ((), ())), preferred_element_type=f32
        )
        dmixed = jnp.concatenate([db, dc], axis=1) * silu_slope(mixed, gate)
        dvalues, rows = convolve_back(dmixed, values, taps_shared_ref[0:4], near)
        at = dproj_ref.shape[1] - 3 * STATE
        drows_ref[0, :, at : at + 2 * STATE] = jnp.concatenate(
            rows + [jnp.zeros((3, 2 * STATE), f32)], axis=0
        )
        raw, step, rate, total = steps_of(shared[:, 2 * STATE :], head_ref[...])
        row, col = positions()
        upper = (row <= col).astype(f32)
        drate = jnp.dot(upper, dtotal[...], precision=highest, preferred_element_type=f32)
        draw = (dstep[...] - drate * head_ref[1:2]) * sigmoid(raw)
        dproj_ref[:, at : at + 2 * STATE] = dvalues.astype(bf16)
        dproj_ref[:, at + 2 * STATE :] = draw.astype(bf16)
        drows_ref[0, :, at + 2 * STATE :] = jnp.concatenate(
            [
                jnp.sum(draw, axis=0, keepdims=True),
                jnp.sum(drate * rate, axis=0, keepdims=True),
                jnp.zeros((6, STATE), f32),
            ],
            axis=0,
        )


def mixer_specs(columns):
    return [
        pl.BlockSpec((LEN, WIDE), lambda s, g: (s, g)),
        pl.BlockSpec((LEN, 3 * STATE), lambda s, g: (s, columns // (3 * STATE))),
        pl.BlockSpec((LEN, 8), lambda s, g: (s, 0)),
        pl.BlockSpec((LEN, 1), lambda s, g: (s, 0)),
        pl.BlockSpec((1, 1, LEN), lambda s, g: (s, 0, 0)),
        pl.BlockSpec((8, WIDE), lambda s, g: (0, g)),
        pl.BlockSpec((8, 2 * STATE), lambda s, g: (0, 0)),
        pl.BlockSpec((8, STATE), lambda s, g: (0, 0)),
    ]


def mixer_scratch(groups):
    return [
        pltpu.VMEM((LEN, LEN), f32),
        pltpu.VMEM((LEN, LEN), f32),
        pltpu.VMEM((groups, LEN, STATE), f32),
        pltpu.VMEM((STATE, LEN), f32),
        pltpu.VMEM((groups, LEN, STATE), f32),
    ]


def mix_forward(proj, near, seg_col, seg_row, taps, taps_shared, heads):
    rows, columns = proj.shape[0], proj.shape[1] - 3 * STATE
    groups = columns // WIDE
    return pl.pallas_call(
        mix_forward_kernel,
        grid=(rows // LEN, groups),
        in_specs=mixer_specs(columns),
        out_specs=pl.BlockSpec((LEN, WIDE), lambda s, g: (s, g)),
        out_shape=jax.ShapeDtypeStruct((rows, columns), f32),
        scratch_shapes=mixer_scratch(groups),
        compiler_params=pltpu.CompilerParams(vmem_limit_bytes=VMEM),
        cost_estimate=pl.CostEstimate(flops=10**9, bytes_accessed=8 * 2**20, transcendentals=10**7),
        name="mix_forward",
    )(proj, proj, near, seg_col, seg_row, taps, taps_shared, heads)


def mix_backward(proj, near, seg_col, seg_row, taps, taps_shared, heads, ssd, dssd):
    rows, columns = proj.shape[0], proj.shape[1] - 3 * STATE
    groups, seqs = columns // WIDE, rows // LEN
    wide = pl.BlockSpec((LEN, WIDE), lambda s, g: (s, g))
    return pl.pallas_call(
        mix_backward_kernel,
        grid=(seqs, groups),
        in_specs=mixer_specs(columns) + [wide, wide],
        out_specs=[
            pl.BlockSpec((LEN, columns + 3 * STATE), lambda s, g: (s, 0)),
            pl.BlockSpec((1, 8, columns + 3 * STATE), lambda s, g: (s, 0, 0)),
        ],
        out_shape=[
            jax.ShapeDtypeStruct(proj.shape, bf16),
            jax.ShapeDtypeStruct((seqs, 8, proj.shape[1]), f32),
        ],
        scratch_shapes=mixer_scratch(groups)
        + [
            pltpu.VMEM((LEN, STATE), bf16),
            pltpu.VMEM((LEN, STATE), bf16),
            pltpu.VMEM((LEN, LEN), f32),
            pltpu.VMEM((LEN, STATE), f32),
            pltpu.VMEM((LEN, STATE), f32),
        ],
        compiler_params=pltpu.CompilerParams(vmem_limit_bytes=56 * 2**20),
        cost_estimate=pl.CostEstimate(flops=3 * 10**9, bytes_accessed=12 * 2**20, transcendentals=10**7),
        name="mix_backward",
    )(proj, proj, near, seg_col, seg_row, taps, taps_shared, heads, ssd, dssd)


SMALL = 8


def two_parts(rows):
    high = rows.astype(bf16).astype(f32)
    return [high, rows - high]


OVER_TOKENS = (((0,), (0,)), ((), ()))


def opposite_kernel(left_ref, right_ref, small_ref, extra_ref, upper_ref, lower_ref):
    product = lax.dot_general(
        left_ref[...], right_ref[...], OVER_TOKENS, preferred_element_type=f32
    )
    small = two_parts(small_ref[0] + small_ref[1] + extra_ref[...])
    half = lower_ref.shape[0]
    upper_ref[...] = jnp.concatenate([product[:half]] + small, axis=0).astype(bf16)
    lower_ref[...] = product[half:].astype(bf16)


def opposite_piece(left, right, small, extra):
    rows, columns = left.shape[1] // SIDE, right.shape[1]
    wide = columns // 3
    return pl.pallas_call(
        opposite_kernel,
        grid=(3,),
        in_specs=[
            pl.BlockSpec((left.shape[0], rows), lambda j: (0, 2)),
            pl.BlockSpec((right.shape[0], wide), lambda j: (0, j)),
            pl.BlockSpec((2, SMALL, wide), lambda j: (0, 0, j)),
            pl.BlockSpec((SMALL, wide), lambda j: (0, j)),
        ],
        out_specs=[
            pl.BlockSpec((rows // 2 + 2 * SMALL, wide), lambda j: (0, j)),
            pl.BlockSpec((rows // 2, wide), lambda j: (0, j)),
        ],
        out_shape=[
            jax.ShapeDtypeStruct((rows // 2 + 2 * SMALL, columns), bf16),
            jax.ShapeDtypeStruct((rows // 2, columns), bf16),
        ],
        compiler_params=pltpu.CompilerParams(vmem_limit_bytes=VMEM),
        cost_estimate=pl.CostEstimate(
            flops=2 * rows * columns * left.shape[0], bytes_accessed=4 * 2**20, transcendentals=0
        ),
        name="opposite_piece",
    )(left, right, small, extra)


def pieces_kernel(
    own_left_ref, after_left_ref, before_left_ref, right_ref, small_ref, extra_ref, late_ref,
    upper_ref, lower_ref, own_ref, after_ref, before_ref,
):
    half, rows = lower_ref.shape[0], 2 * lower_ref.shape[0]
    small = small_ref[0] + small_ref[1] + extra_ref[...] + late_ref[...]
    upper = upper_ref[...].astype(f32)
    passed = upper[half : half + SMALL] + upper[half + SMALL :]
    nothing = jnp.zeros((half, small.shape[1]), f32)
    times = lambda ref: lax.dot_general(
        ref[...], right_ref[...], OVER_TOKENS, preferred_element_type=f32
    )
    own_ref[...] = jnp.concatenate([times(own_left_ref), small, jnp.zeros_like(small)], axis=0)
    after = times(after_left_ref) + jnp.concatenate([upper[:half], nothing], axis=0)
    after_ref[...] = jnp.concatenate([after] + two_parts(small + passed), axis=0).astype(bf16)
    before = times(before_left_ref) + jnp.concatenate(
        [nothing, lower_ref[...].astype(f32)], axis=0
    )
    before_ref[...] = jnp.concatenate([before] + two_parts(small), axis=0).astype(bf16)


def other_pieces(left, right, small, extra, late, upper, lower):
    rows, columns = left.shape[1] // SIDE, right.shape[1]
    wide = columns // 3
    piece = lambda k: pl.BlockSpec((left.shape[0], rows), lambda j: (0, k))
    block = lambda height: pl.BlockSpec((height, wide), lambda j: (0, j))
    total = rows + 2 * SMALL
    return pl.pallas_call(
        pieces_kernel,
        grid=(3,),
        in_specs=[
            piece(0),
            piece(1),
            piece(3),
            block(right.shape[0]),
            pl.BlockSpec((2, SMALL, wide), lambda j: (0, 0, j)),
            block(SMALL),
            block(SMALL),
            block(upper.shape[0]),
            block(lower.shape[0]),
        ],
        out_specs=[block(total)] * 3,
        out_shape=[
            jax.ShapeDtypeStruct((total, columns), f32),
            jax.ShapeDtypeStruct((total, columns), bf16),
            jax.ShapeDtypeStruct((total, columns), bf16),
        ],
        compiler_params=pltpu.CompilerParams(vmem_limit_bytes=VMEM),
        cost_estimate=pl.CostEstimate(
            flops=6 * rows * columns * left.shape[0], bytes_accessed=9 * 2**20, transcendentals=0
        ),
        name="other_pieces",
    )(left, left, left, right, small, extra, late, upper, lower)


def normed_kernel(
    core_ref, places_ref, dgate_ref, gate_ref, dproj_ref, normed_ref, gain_ref, *refs
):
    mix_refs = refs[:SIDE]
    own_ref, other_ref, row_ref, total = refs[SIDE:]
    step = pl.program_id(0)
    core = core_ref[0]
    turned = (((1,), (1,)), ((), ()))
    wide, width = gate_ref.shape[0], total.shape[1]
    spots = lax.broadcasted_iota(jnp.int32, (width, wide), 0)
    reorder = (spots == places_ref[...]).astype(f32).astype(bf16)
    for k, ref in enumerate(mix_refs):

        @pl.when(step == k)
        def _(k=k, ref=ref):
            back = lax.dot_general(dproj_ref[...], ref[...], turned, preferred_element_type=f32)
            back = lax.dot_general(
                back.astype(bf16), reorder, turned, preferred_element_type=f32
            )
            if k == 0:
                total[...] = back
            else:
                total[...] += back

    at = pl.ds(pl.multiple_of(step * wide, wide), wide)
    total[:, at] += lax.dot_general(dgate_ref[...], gate_ref[...], turned, preferred_element_type=f32)

    @pl.when(step == SIDE - 1)
    def _():
        own_ref[...] = total[pl.ds(pl.multiple_of(core * LEN, LEN), LEN), :]
        other = total[pl.ds(pl.multiple_of((1 - core) * LEN, LEN), LEN), :]
        other_ref[...] = other.astype(bf16)
        gain = jnp.sum(total[...] * normed_ref[...].astype(f32), axis=0, keepdims=True)
        gain = jnp.concatenate(
            [gain / gain_ref[...], jnp.zeros((1, row_ref.shape[1] - width), f32)], axis=1
        )
        row = lax.broadcasted_iota(jnp.int32, row_ref.shape, 0)
        row_ref[...] = jnp.where(row == SMALL - 1, gain, 0.0)


def normed_parts(core, places, dgate, w_rest, dproj, normed, gain, w_mix):
    rows, width = dgate.shape[0], places.shape[1]
    wide = width // SIDE
    full = lambda array: pl.BlockSpec(array.shape, lambda j: (0, 0))
    return pl.pallas_call(
        normed_kernel,
        grid=(SIDE,),
        in_specs=[
            pl.BlockSpec(memory_space=pltpu.SMEM),
            pl.BlockSpec((1, wide), lambda j: (0, j)),
            full(dgate),
            pl.BlockSpec((wide, dgate.shape[1]), lambda j: (j, 0)),
            full(dproj),
            full(normed),
            full(gain),
        ]
        + [full(piece) for piece in w_mix],
        out_specs=[pl.BlockSpec((LEN, width), lambda j: (0, 0))] * 2
        + [pl.BlockSpec((SMALL, dproj.shape[1]), lambda j: (0, 0))],
        out_shape=[
            jax.ShapeDtypeStruct((LEN, width), f32),
            jax.ShapeDtypeStruct((LEN, width), bf16),
            jax.ShapeDtypeStruct((SMALL, dproj.shape[1]), f32),
        ],
        scratch_shapes=[pltpu.VMEM((rows, width), f32)],
        compiler_params=pltpu.CompilerParams(vmem_limit_bytes=56 * 2**20),
        cost_estimate=pl.CostEstimate(
            flops=10**10, bytes_accessed=24 * 2**20, transcendentals=0
        ),
        name="normed_parts",
    )(core, places, dgate, w_rest, dproj, normed, gain, *w_mix)


def branch_kernel(core_ref, own_mixed_ref, other_mixed_ref, out_ref, own_ref, other_ref, total):
    step = pl.program_id(0)
    core = core_ref[0]
    mixed = jnp.where(step // (SIDE // 2) == core, own_mixed_ref[...], other_mixed_ref[...])
    part = jnp.dot(mixed, out_ref[...], preferred_element_type=f32)

    @pl.when(step == 0)
    def _():
        total[...] = part

    @pl.when(step > 0)
    def _():
        total[...] += part

    @pl.when(step == SIDE - 1)
    def _():
        own_ref[...] = total[pl.ds(pl.multiple_of(core * LEN, LEN), LEN), :].astype(bf16)
        other = total[pl.ds(pl.multiple_of((1 - core) * LEN, LEN), LEN), :]
        other_ref[...] = other.astype(bf16)


def branch_parts(core, own_mixed, other_mixed, w_out):
    rows, half, width = own_mixed.shape[0], own_mixed.shape[1], w_out.shape[1]
    deep = 2 * half // SIDE
    mixed = pl.BlockSpec((rows, deep), lambda j: (0, j % (SIDE // 2)))
    return pl.pallas_call(
        branch_kernel,
        grid=(SIDE,),
        in_specs=[
            pl.BlockSpec(memory_space=pltpu.SMEM),
            mixed,
            mixed,
            pl.BlockSpec((deep, width), lambda j: (j, 0)),
        ],
        out_specs=[pl.BlockSpec((LEN, width), lambda j: (0, 0))] * 2,
        out_shape=[jax.ShapeDtypeStruct((LEN, width), bf16)] * 2,
        scratch_shapes=[pltpu.VMEM((rows, width), f32)],
        compiler_params=pltpu.CompilerParams(vmem_limit_bytes=56 * 2**20),
        cost_estimate=pl.CostEstimate(
            flops=4 * rows * half * width, bytes_accessed=9 * 2**20, transcendentals=0
        ),
        name="branch_parts",
    )(core, own_mixed, other_mixed, w_out)


def fold_kernel(*refs):
    late_ref, in_refs, out_refs = refs[0], refs[1:-SIDE], refs[-SIDE:]
    kept = (in_refs[0].shape[0] - 2 * SMALL) // 16 * 16
    part = kept // SIDE
    small = late_ref[...]
    for ref in in_refs:
        tail = ref[kept : kept + 2 * SMALL].astype(f32)
        small = small + tail[:SMALL] + tail[SMALL:]
    fill = out_refs[0].shape[0] - part - 2 * SMALL
    fill = [jnp.zeros((fill, small.shape[1]), f32)] if fill else []
    for k, out_ref in enumerate(out_refs):
        total = sum(ref[k * part : (k + 1) * part].astype(f32) for ref in in_refs)
        below = [small, jnp.zeros_like(small)] if k == 0 else two_parts(small)
        out_ref[...] = jnp.concatenate([total] + below + fill, axis=0).astype(out_ref.dtype)


def fold(arrays, late):
    held, columns = arrays[0].shape
    rows = -(-((held - 2 * SMALL) // 16 * 16 // SIDE + 2 * SMALL) // 16) * 16
    steps = 5
    block = lambda height: pl.BlockSpec((height, columns // steps), lambda j: (0, j))
    return pl.pallas_call(
        fold_kernel,
        grid=(steps,),
        in_specs=[block(SMALL)] + [block(held)] * len(arrays),
        out_specs=[block(rows)] * SIDE,
        out_shape=[
            jax.ShapeDtypeStruct((rows, columns), bf16 if k else f32) for k in range(SIDE)
        ],
        compiler_params=pltpu.CompilerParams(vmem_limit_bytes=VMEM),
        cost_estimate=pl.CostEstimate(flops=10**7, bytes_accessed=8 * 2**20, transcendentals=0),
        name="fold",
    )(late, *arrays)


def owners_kernel(core_ref, own_ref, other_ref, cot_ref, normed_ref, dgate_ref, out_ref):
    shards, width = out_ref.shape[0], out_ref.shape[2]
    mine = pl.program_id(0) // (pl.num_programs(0) // 2) == core_ref[0]
    mixed = jnp.where(mine, own_ref[...], other_ref[...])
    grad_out = lax.dot_general(
        mixed, cot_ref[...], OVER_TOKENS, preferred_element_type=f32
    ).reshape(shards, -1, width)
    grad_gate = lax.dot_general(
        normed_ref[...], dgate_ref[...], OVER_TOKENS, preferred_element_type=f32
    )
    grad_gate = grad_gate.reshape(shards, -1, 2 * width)
    out_ref[...] = jnp.concatenate(
        [grad_out, grad_gate[:, :, :width], grad_gate[:, :, width:]], axis=1
    ).astype(bf16)


def owners_grads(core, own, other, cot, normed, dgate, shards):
    steps = 4
    each = shards // steps
    width = cot.shape[1]
    rows_out, rows_in = 2 * own.shape[1] // shards, normed.shape[1] // shards
    mixed = pl.BlockSpec((own.shape[0], each * rows_out), lambda j: (0, j % (steps // 2)))
    rows = rows_out + 2 * rows_in
    return pl.pallas_call(
        owners_kernel,
        grid=(steps,),
        in_specs=[
            pl.BlockSpec(memory_space=pltpu.SMEM),
            mixed,
            mixed,
            pl.BlockSpec(cot.shape, lambda j: (0, 0)),
            pl.BlockSpec((normed.shape[0], each * rows_in), lambda j: (0, j)),
            pl.BlockSpec(dgate.shape, lambda j: (0, 0)),
        ],
        out_specs=pl.BlockSpec((each, rows, width), lambda j: (j, 0, 0)),
        out_shape=pltpu.HBM((shards, rows, width), bf16),
        compiler_params=pltpu.CompilerParams(vmem_limit_bytes=VMEM),
        cost_estimate=pl.CostEstimate(
            flops=2 * cot.shape[0] * shards * rows * width, bytes_accessed=16 * 2**20, transcendentals=0
        ),
        name="owners_grads",
    )(core, own, other, cot, normed, dgate)


CHIPS = ("z", "y", "x")
ALL = ("grp",) + CHIPS
SIDE = 4
ORDERS = (("x", "y", "z"), ("y", "z", "x"))
GRAD_ORDERS = (("x", "y", "z"), ("x", "z", "y"))


def place(core, spot):
    index = core
    for axis in CHIPS:
        index = index * SIDE + spot[axis] % SIDE
    return index


def moved(value, phase, by, orders=GRAD_ORDERS):
    pairs = []
    for core in range(2):
        for z in range(SIDE):
            for y in range(SIDE):
                for x in range(SIDE):
                    spot = dict(z=z, y=y, x=x)
                    axis = orders[core][phase]
                    pairs.append((place(core, spot), place(core, {**spot, axis: spot[axis] + by})))
    return lax.ppermute(value, ALL, pairs)


def along(value, axis, by):
    return lax.ppermute(value, axis, [(i, (i + by) % SIDE) for i in range(SIDE)])


def swapped(value):
    return lax.ppermute(value, "grp", [(0, 1), (1, 0)])


def in_order(own, other, axis=0):
    first = lax.axis_index("grp") == 0
    return jnp.concatenate([jnp.where(first, own, other), jnp.where(first, other, own)], axis=axis)


def turned(value, dim, by):
    twice = jnp.concatenate([value, value], axis=dim)
    return lax.dynamic_slice_in_dim(twice, by, value.shape[dim], dim)


def gathered(own, orders, later):
    for phase in (2, 1):
        own = jnp.concatenate([own] + [moved(own, phase, -k, orders) for k in range(1, SIDE)])
    own, later = lax.optimization_barrier((own, later))
    after, before = moved(own, 0, -1, orders), moved(own, 0, 1, orders)
    middle = own.shape[0] // 2
    opposite = [moved(after[:middle], 0, -1, orders), moved(before[middle:], 0, 1, orders)]
    return [own, after, jnp.concatenate(opposite), before], later


def row_places(rows, orders):
    index = lax.iota(jnp.int32, SIDE**3 * rows)
    steps = (index // (SIDE * SIDE * rows), index // (SIDE * rows) % SIDE, index // rows % SIDE)
    core = lax.axis_index("grp")
    places = []
    for order in orders:
        spot = {axis: (lax.axis_index(axis) + step) % SIDE for axis, step in zip(order, steps)}
        places.append(((spot["z"] * SIDE + spot["y"]) * SIDE + spot["x"]) * rows + index % rows)
    return jnp.where(core == 0, places[0], places[1])


def halved(array, size, dim, other=False):
    core = lax.axis_index("grp")
    return lax.dynamic_slice_in_dim(array, (1 - core if other else core) * size, size, dim)


def times(left, right):
    return jnp.dot(left, right, preferred_element_type=f32)


def times_turned(left, right):
    return lax.dot_general(left, right, (((1,), (1,)), ((), ())), preferred_element_type=f32)


def on_device(
    tokens,
    segment_ids,
    norm_gain,
    in_weight,
    conv_weight,
    conv_bias,
    dt_bias,
    a_log,
    skip_d,
    gnorm_gain,
    out_weight,
    cotangent,
):
    width = tokens.shape[1]
    inner = gnorm_gain.shape[0]
    half = inner // 2
    heads = dt_bias.shape[0] // 2
    bc = conv_bias.shape[0] - inner
    rows_in, rows_out = in_weight.shape[0], out_weight.shape[0]
    shards = SIDE**3

    own_mix = jnp.concatenate(
        [
            halved(in_weight[:, inner : 2 * inner], half, 1),
            in_weight[:, 2 * inner : 2 * inner + bc],
            halved(in_weight[:, inner + inner + bc :], heads, 1),
            jnp.zeros((rows_in, STATE - heads), bf16),
        ],
        axis=1,
    )
    own_out = halved(out_weight, width // 2, 1)
    own_rest = jnp.concatenate(
        [halved(in_weight[:, :inner], half, 1), own_out[:rows_in], own_out[rows_in:]], axis=1
    )
    w_rest = lax.all_gather(own_rest, CHIPS, axis=0, tiled=True)
    w_mix, places = gathered(own_mix, ORDERS, row_places(rows_in, ORDERS))

    residual = tokens.astype(f32)
    scale = lax.rsqrt(jnp.mean(residual * residual, axis=-1, keepdims=True) + NORM_EPS)
    unit = residual * scale
    own_low = (unit * norm_gain).astype(bf16)
    normed = in_order(own_low, swapped(own_low))
    cot = in_order(cotangent, swapped(cotangent))
    segments = in_order(segment_ids, swapped(segment_ids))
    near = [jnp.zeros(segments.shape, f32)]
    for back in range(1, TAPS):
        same = (segments[:, back:] == segments[:, :-back]).astype(f32)
        near.append(jnp.pad(same, ((0, 0), (back, 0))))
    near = jnp.stack(near + [near[0]] * 4, axis=-1).reshape(-1, 8)
    seg_col = segments.astype(f32).reshape(-1, 1)
    seg_row = segments.astype(f32)[:, None, :]

    taps = jnp.concatenate(
        [
            halved(conv_weight[:, :inner], half, 1),
            halved(conv_bias[None, :inner], half, 1),
            jnp.repeat(halved(skip_d, heads, 0), HEAD)[None],
            halved(gnorm_gain[None], half, 1),
            jnp.zeros((1, half), f32),
        ]
    )
    taps_shared = jnp.concatenate(
        [conv_weight[:, inner:], conv_bias[None, inner:], jnp.zeros((3, bc), f32)]
    )
    head_rows = jnp.stack([halved(dt_bias, heads, 0), jnp.exp(halved(a_log, heads, 0))])
    head_rows = jnp.pad(head_rows, ((0, 6), (0, STATE - heads)))
    gain = halved(gnorm_gain, half, 0)

    reorder = (lax.iota(jnp.int32, width)[:, None] == places[None, :]).astype(bf16)
    normed_moved = times(normed, reorder).astype(bf16)
    reorder = (
        lax.iota(jnp.int32, width)[:, None] == row_places(rows_in, GRAD_ORDERS)[None, :]
    ).astype(bf16)
    left = times(normed, reorder).astype(bf16)
    cot_half = halved(cot, width // 2, 1)

    core = lax.axis_index("grp")
    which = core.astype(jnp.int32)[None]
    quarter = width // SIDE
    proj = sum(
        times(normed_moved[:, k * quarter : (k + 1) * quarter], w_mix[k]) for k in range(SIDE)
    )
    sides = (near, seg_col, seg_row, taps, taps_shared, head_rows)
    ssd = mix_forward(proj, *sides)
    ssd, w_rest, cot_half, normed, left = lax.optimization_barrier(
        (ssd, w_rest, cot_half, normed, left)
    )
    w_out = jnp.stack(
        [
            w_rest[:, half : half + width // 2].reshape(shards, rows_in, -1),
            w_rest[:, half + width // 2 :].reshape(shards, rows_in, -1),
        ],
        axis=1,
    ).reshape(inner, -1)
    mixer_parts = times_turned(cot_half, w_out).astype(bf16)
    mixer_parts, normed = lax.optimization_barrier((mixer_parts, normed))
    gate_part = times(normed, w_rest[:, :half])
    grad_mixer = halved(mixer_parts, half, 1), swapped(halved(mixer_parts, half, 1, other=True))
    gate_part, grad_mixer = lax.optimization_barrier((gate_part, grad_mixer))
    grad_mixer = grad_mixer[0].astype(f32) + grad_mixer[1].astype(f32)
    opening = sigmoid(gate_part)
    gate = gate_part * opening
    gated = ssd * gate
    weighted = grad_mixer * gain
    sums = jnp.stack([jnp.sum(gated * gated, axis=-1), jnp.sum(gated * weighted, axis=-1)])
    sums = sums + swapped(sums)
    gscale = lax.rsqrt(sums[0] / inner + NORM_EPS)[:, None]
    pull = gscale * gscale * gscale * (sums[1] / inner)[:, None]
    mixer_low = (gated * gscale * gain).astype(bf16)
    mixer_low, ssd, gate_part, grad_mixer, gscale, pull = lax.optimization_barrier(
        (mixer_low, ssd, gate_part, grad_mixer, gscale, pull)
    )
    mixer_other = swapped(mixer_low)
    opening = sigmoid(gate_part)
    gate = gate_part * opening
    gated = ssd * gate
    dgated = gscale * (grad_mixer * gain) - gated * pull
    grad_gain = jnp.sum(grad_mixer * gated * gscale, axis=0)
    dgate_low = (dgated * ssd * silu_slope(gate_part, opening)).astype(bf16)
    dssd = (dgated * gate).astype(bf16)

    rest_grad = owners_grads(which, mixer_low, mixer_other, cot_half, normed, dgate_low, shards)
    rest_rows = rest_grad.shape[1]
    gain_row = jnp.zeros((SMALL, proj.shape[1]), f32).at[6, :half].set(grad_gain)
    rest_grad, dssd, gain_row = lax.optimization_barrier((rest_grad, dssd, gain_row))
    rest_share = lax.psum_scatter(
        rest_grad.reshape(shards * rest_rows, -1), ("z", "y"), scatter_dimension=0, tiled=True
    )

    dproj, drows = mix_backward(proj, *sides, ssd, dssd)
    leaving = (left, dproj, drows, gain_row)
    upper, lower = opposite_piece(*leaving)

    dproj, upper, lower = lax.optimization_barrier((dproj, upper, lower))
    halves_here = moved(upper, 0, 1), moved(lower, 0, -1)
    normed_own, normed_other, late = normed_parts(
        which, places[None], dgate_low, w_rest, dproj, normed, norm_gain[None], w_mix
    )
    halves_here, late = lax.optimization_barrier((halves_here, late))
    own, after, before = other_pieces(*leaving, late, *halves_here)
    mixer_low, after, before, late = lax.optimization_barrier((mixer_low, after, before, late))
    received = [own, moved(after, 0, 1), moved(before, 0, -1)]
    late = moved(late, 0, 2)
    branch_own, branch_other = branch_parts(which, mixer_low, mixer_other, w_out)
    received, branch_own = lax.optimization_barrier((received, branch_own))
    own, *gone = fold(received, late)
    own, *gone = fold([own] + [moved(gone[k - 1], 1, k) for k in range(1, SIDE)], jnp.zeros_like(late))
    rest_turned = turned(rest_share.reshape(SIDE, rest_rows, -1), 0, lax.axis_index("x"))
    gone, rest_turned = lax.optimization_barrier((gone, rest_turned))
    rest_total = rest_turned[0].astype(f32) + sum(
        along(rest_turned[k], "x", k).astype(f32) for k in range(1, SIDE)
    )
    mix_total = own + sum(moved(gone[k - 1], 2, k).astype(f32) for k in range(1, SIDE))
    mix_share = mix_total[:rows_in]
    small = mix_total[rows_in : rows_in + SMALL] + mix_total[rows_in + SMALL : rows_in + 2 * SMALL]

    branch = in_order(branch_own, swapped(branch_other), axis=1)
    out_tokens = (residual + branch.astype(f32)).astype(bf16)
    grad_normed = normed_own + swapped(normed_other).astype(f32)
    q = grad_normed * norm_gain
    grad_tokens = cotangent.astype(f32) + scale * (
        q - unit * jnp.mean(q * unit, axis=-1, keepdims=True)
    )
    small_other = swapped(small)
    mix_other, rest_other = swapped(mix_share), swapped(rest_total)
    bc_sum = (mix_share + mix_other)[:, half : half + bc]
    dt_at = slice(half + bc, half + bc + heads)
    ends = rows_out, rows_out + rows_in, rows_out + 2 * rows_in
    gate_total, gate_other = (
        jnp.concatenate([rest[ends[0] : ends[1]], rest[ends[1] : ends[2]]], axis=1)
        for rest in (rest_total, rest_other)
    )
    grad_in_weight = jnp.concatenate(
        [
            in_order(gate_total, gate_other, axis=1),
            in_order(mix_share[:, :half], mix_other[:, :half], axis=1),
            bc_sum,
            in_order(mix_share[:, dt_at], mix_other[:, dt_at], axis=1),
        ],
        axis=1,
    )
    grad_out_weight = in_order(rest_total[:rows_out], rest_other[:rows_out], axis=1)
    both = in_order(small[:, :half], small_other[:, :half], axis=1)
    summed = small + small_other
    shared_rows = summed[:, half : half + bc]
    head_sums = in_order(small[:, dt_at], small_other[:, dt_at], axis=1)
    return (
        out_tokens,
        grad_tokens,
        summed[SMALL - 1, :width],
        grad_in_weight,
        jnp.concatenate([both[:4], shared_rows[:4]], axis=1),
        jnp.concatenate([both[4], shared_rows[4]]),
        head_sums[0],
        head_sums[1],
        both[5].reshape(-1, HEAD).sum(axis=-1),
        both[6],
        grad_out_weight,
    )


def solution(mesh):
    chips = Mesh(mesh.devices.reshape(2, SIDE, SIDE, SIDE), ALL)
    rows = P(ALL, None)
    owned = P(CHIPS, None)
    return jax.shard_map(
        on_device,
        mesh=chips,
        in_specs=(rows, rows, P(), owned, P(), P(), P(), P(), P(), P(), owned, rows),
        out_specs=(rows, rows, P(), owned, P(), P(), P(), P(), P(), P(), owned),
        check_vma=False,
    )
```

```python
import functools

import jax
import jax.numpy as jnp
import numpy as np
from jax import lax
from jax.experimental import pallas as pl
from jax.experimental.pallas import tpu as pltpu
from jax.sharding import Mesh
from jax.sharding import PartitionSpec as P

LEN = 256
VMEM = 24 * 2**20
WHOLE_VMEM = 56 * 2**20
HALF = 128
HEAD = 64
GROUP = 8
WIDE = GROUP * HEAD
STATE = 128
TAPS = 4
NORM_EPS = 1e-05
LOG2E = 1.4426950408889634
FAR = -1e30
bf16 = jnp.bfloat16
f32 = jnp.float32
highest = lax.Precision.HIGHEST


def sigmoid(v):
    return 0.5 + 0.5 * jnp.tanh(0.5 * v)


def convolve(values, taps, bias, near):
    total = bias + taps[TAPS - 1 : TAPS] * values
    for back in range(1, TAPS):
        tap = taps[TAPS - 1 - back : TAPS - back]
        total = total + tap * (near[:, back : back + 1] * pltpu.roll(values, back, 0))
    return total


def convolve_back(grad, values, taps, near):
    total = taps[TAPS - 1 : TAPS] * grad
    rows = [jnp.sum(grad * values, axis=0, keepdims=True)]
    for back in range(1, TAPS):
        tap = taps[TAPS - 1 - back : TAPS - back]
        seen = pltpu.roll(near[:, back : back + 1] * grad, LEN - back, 0)
        total = total + tap * seen
        rows.append(jnp.sum(seen * values, axis=0, keepdims=True))
    return total, rows[::-1] + [jnp.sum(grad, axis=0, keepdims=True)]


def silu_slope(v, s):
    return s * (1.0 + v * (1.0 - s))


def positions():
    return (
        lax.broadcasted_iota(jnp.int32, (LEN, LEN), 0),
        lax.broadcasted_iota(jnp.int32, (LEN, LEN), 1),
    )


def softplus(v):
    small = jnp.exp(-jnp.abs(v))
    return jnp.maximum(v, 0.0) + jnp.log1p(small)


def steps_of(dt_part, head_rows):
    raw = dt_part + head_rows[0:1]
    step = softplus(raw)
    rate = -step * head_rows[1:2]
    row, col = positions()
    lower = (row >= col).astype(f32)
    total = jnp.dot(lower, rate, precision=highest, preferred_element_type=f32) * LOG2E
    return raw, step, rate, total


def split_dot(values, ones):
    high = values.astype(bf16)
    low = (values - high.astype(f32)).astype(bf16)
    return jnp.dot(high, ones, preferred_element_type=f32) + jnp.dot(
        low, ones, preferred_element_type=f32
    )


def pair_columns(table, pair):
    lane = lax.broadcasted_iota(jnp.int32, (LEN, 2 * HEAD), 1)
    return jnp.where(lane < HEAD, table[:, 2 * pair : 2 * pair + 1], table[:, 2 * pair + 1 : 2 * pair + 2])


def pair_of(both):
    lane = lax.broadcasted_iota(jnp.int32, (LEN, 2 * HEAD), 1)
    return jnp.where(lane < HEAD, both[:LEN], both[LEN:])


def halves(values):
    lane = lax.broadcasted_iota(jnp.int32, values.shape, 1)
    zero = jnp.zeros_like(values)
    return jnp.where(lane < HEAD, values, zero), jnp.where(lane >= HEAD, values, zero)


def mix_forward_kernel(
    proj_ref, shared_ref, near_ref, seg_col_ref, seg_row_ref, taps_ref, taps_shared_ref, head_ref,
    ssd_ref, mixed_ref, scores, apart, totals, totals_row, steps,
):
    group = pl.program_id(1)
    near = near_ref[...]

    @pl.when(group == 0)
    def _():
        shared = shared_ref[...]
        mixed = convolve(shared[:, : 2 * STATE], taps_shared_ref[0:4], taps_shared_ref[4:5], near)
        mixed = mixed * sigmoid(mixed)
        b_low = mixed[:, :STATE].astype(bf16)
        c_low = mixed[:, STATE:].astype(bf16)
        scores[...] = lax.dot_general(
            c_low, b_low, (((1,), (1,)), ((), ())), preferred_element_type=f32
        )
        row, col = positions()
        seen = (row >= col) & (seg_col_ref[...] == seg_row_ref[0])
        apart[...] = jnp.where(seen, 0.0, FAR)
        raw, step, rate, total = steps_of(shared[:, 2 * STATE :], head_ref[...])
        for g in range(totals.shape[0]):
            turn = (STATE - GROUP * g) % STATE
            totals[g] = pltpu.roll(total, turn, 1) if turn else total
            steps[g] = pltpu.roll(step, turn, 1) if turn else step
        totals_row[...] = total.T

    values = proj_ref[...]
    mixed = convolve(values, taps_ref[0:4], taps_ref[4:5], near)
    mixed_ref[...] = mixed
    x = mixed * sigmoid(mixed)
    total = totals[group]
    step = steps[group]
    total_row = totals_row[pl.ds(pl.multiple_of(group * GROUP, GROUP), GROUP), :]
    skip = taps_ref[5:6]
    for pair in range(GROUP // 2):
        lanes = slice(2 * HEAD * pair, 2 * HEAD * (pair + 1))
        x_pair = x[:, lanes]
        low_x = (pair_columns(step, pair) * x_pair).astype(bf16)
        weights = []
        for head in (2 * pair, 2 * pair + 1):
            col = total[:, head : head + 1]
            row = total_row[head : head + 1, :]
            decay = jnp.exp2(col[:HALF] - row[:, :HALF] + apart[:HALF, :HALF])
            weight = (scores[:HALF, :HALF] * decay).astype(bf16)
            weights.append(jnp.concatenate([weight, jnp.zeros_like(weight)], axis=1))
            decay = jnp.exp2(col[HALF:] - row + apart[HALF:, :])
            weights.append((scores[HALF:, :] * decay).astype(bf16))
        both = jnp.dot(jnp.concatenate(weights, axis=0), low_x, preferred_element_type=f32)
        inside = pair_of(both)
        ssd_ref[:, lanes] = inside + skip[:, lanes] * x_pair


def mix_backward_kernel(
    proj_ref, shared_ref, near_ref, seg_col_ref, seg_row_ref, taps_ref, taps_shared_ref, head_ref,
    ssd_ref, dssd_ref, mixed_ref,
    dproj_ref, drows_ref,
    scores, apart, totals, totals_row, steps, b_keep, c_keep, dscores, dtotal, dstep,
):
    group = pl.program_id(1)
    last = pl.num_programs(1) - 1
    near = near_ref[...]

    @pl.when(group == 0)
    def _():
        shared = shared_ref[...]
        mixed = convolve(shared[:, : 2 * STATE], taps_shared_ref[0:4], taps_shared_ref[4:5], near)
        mixed = mixed * sigmoid(mixed)
        b_low = mixed[:, :STATE].astype(bf16)
        c_low = mixed[:, STATE:].astype(bf16)
        b_keep[...] = b_low
        c_keep[...] = c_low
        scores[...] = lax.dot_general(
            b_low, c_low, (((1,), (1,)), ((), ())), preferred_element_type=f32
        )
        row, col = positions()
        seen = (row <= col) & (seg_col_ref[...] == seg_row_ref[0])
        apart[...] = jnp.where(seen, 0.0, FAR)
        raw, step, rate, total = steps_of(shared[:, 2 * STATE :], head_ref[...])
        for g in range(totals.shape[0]):
            turn = (STATE - GROUP * g) % STATE
            totals[g] = pltpu.roll(total, turn, 1) if turn else total
            steps[g] = pltpu.roll(step, turn, 1) if turn else step
        totals_row[...] = total.T
        dscores[...] = jnp.zeros_like(dscores)
        dtotal[...] = jnp.zeros_like(dtotal)
        dstep[...] = jnp.zeros_like(dstep)

    values = proj_ref[...]
    mixed = mixed_ref[...]
    gate = sigmoid(mixed)
    x = mixed * gate
    total = totals[group]
    step = steps[group]
    total_row = totals_row[pl.ds(pl.multiple_of(group * GROUP, GROUP), GROUP), :]
    skip = taps_ref[5:6]
    dx_parts, total_parts, step_parts, skip_parts = [], [], [], []
    for pair in range(GROUP // 2):
        lanes = slice(2 * HEAD * pair, 2 * HEAD * (pair + 1))
        x_pair = x[:, lanes]
        dt_pair = pair_columns(step, pair)
        low_x = (dt_pair * x_pair).astype(bf16)
        low_dy = dssd_ref[:, lanes]
        dy = low_dy.astype(f32)
        weights, decays = [], []
        for head in (2 * pair, 2 * pair + 1):
            col = total[:, head : head + 1]
            row = total_row[head : head + 1, :]
            decays.append(jnp.exp2(row - col[:HALF] + apart[:HALF, :]))
            weights.append((scores[:HALF, :] * decays[-1]).astype(bf16))
            decays.append(jnp.exp2(row[:, HALF:] - col[HALF:] + apart[HALF:, HALF:]))
            weight = (scores[HALF:, HALF:] * decays[-1]).astype(bf16)
            weights.append(jnp.concatenate([jnp.zeros_like(weight), weight], axis=1))
        back = jnp.dot(jnp.concatenate(weights, axis=0), low_dy, preferred_element_type=f32)
        back = pair_of(back)
        grads = lax.dot_general(
            jnp.concatenate(halves(low_x), axis=0), low_dy, (((1,), (1,)), ((), ())),
            preferred_element_type=f32,
        )
        dscores[:HALF, :] += grads[:HALF] * decays[0] + grads[LEN : LEN + HALF] * decays[2]
        dscores[HALF:, HALF:] += (
            grads[HALF:LEN, HALF:] * decays[1] + grads[LEN + HALF :, HALF:] * decays[3]
        )
        skip_pair = skip[:, lanes]
        inside = ssd_ref[:, lanes] - skip_pair * x_pair
        total_parts.append(dy * inside - low_x.astype(f32) * back)
        step_parts.append(x_pair * back)
        skip_parts.append(jnp.sum(dy * x_pair, axis=0, keepdims=True))
        dx_parts.append(dt_pair * back + skip_pair * dy)
    wide = lambda parts: jnp.concatenate(parts, axis=1)
    place = lax.broadcasted_iota(jnp.int32, (WIDE, STATE), 0) // HEAD + group * GROUP
    ones = (place == lax.broadcasted_iota(jnp.int32, (WIDE, STATE), 1)).astype(bf16)
    dtotal[...] += split_dot(wide(total_parts), ones)
    dstep[...] += jnp.dot(wide(step_parts).astype(bf16), ones, preferred_element_type=f32)
    dmixed = wide(dx_parts) * silu_slope(mixed, gate)
    dvalues, rows = convolve_back(dmixed, values, taps_ref[0:4], near)
    dproj_ref[:, pl.ds(pl.multiple_of(group * WIDE, WIDE), WIDE)] = dvalues.astype(bf16)
    drows_ref[0, :, pl.ds(pl.multiple_of(group * WIDE, WIDE), WIDE)] = jnp.concatenate(
        rows + [wide(skip_parts), jnp.zeros((2, WIDE), f32)], axis=0
    )

    @pl.when(group == last)
    def _():
        shared = shared_ref[...]
        values = shared[:, : 2 * STATE]
        mixed = convolve(values, taps_shared_ref[0:4], taps_shared_ref[4:5], near)
        gate = sigmoid(mixed)
        low = dscores[...].astype(bf16)
        db = jnp.dot(low, c_keep[...], preferred_element_type=f32)
        dc = lax.dot_general(
            low, b_keep[...], (((0,), (0,)), ((), ())), preferred_element_type=f32
        )
        dmixed = jnp.concatenate([db, dc], axis=1) * silu_slope(mixed, gate)
        dvalues, rows = convolve_back(dmixed, values, taps_shared_ref[0:4], near)
        at = dproj_ref.shape[1] - 3 * STATE
        drows_ref[0, :, at : at + 2 * STATE] = jnp.concatenate(
            rows + [jnp.zeros((3, 2 * STATE), f32)], axis=0
        )
        raw, step, rate, total = steps_of(shared[:, 2 * STATE :], head_ref[...])
        row, col = positions()
        upper = (row <= col).astype(f32)
        drate = jnp.dot(upper, dtotal[...], precision=highest, preferred_element_type=f32)
        draw = (dstep[...] - drate * head_ref[1:2]) * sigmoid(raw)
        dproj_ref[:, at : at + 2 * STATE] = dvalues.astype(bf16)
        dproj_ref[:, at + 2 * STATE :] = draw.astype(bf16)
        drows_ref[0, :, at + 2 * STATE :] = jnp.concatenate(
            [
                jnp.sum(draw, axis=0, keepdims=True),
                jnp.sum(drate * rate, axis=0, keepdims=True),
                jnp.zeros((6, STATE), f32),
            ],
            axis=0,
        )


def mixer_specs(columns):
    return [
        pl.BlockSpec((LEN, WIDE), lambda s, g: (s, g)),
        pl.BlockSpec((LEN, 3 * STATE), lambda s, g: (s, columns // (3 * STATE))),
        pl.BlockSpec((LEN, 8), lambda s, g: (s, 0)),
        pl.BlockSpec((LEN, 1), lambda s, g: (s, 0)),
        pl.BlockSpec((1, 1, LEN), lambda s, g: (s, 0, 0)),
        pl.BlockSpec((8, WIDE), lambda s, g: (0, g)),
        pl.BlockSpec((8, 2 * STATE), lambda s, g: (0, 0)),
        pl.BlockSpec((8, STATE), lambda s, g: (0, 0)),
    ]


def mixer_scratch(groups):
    return [
        pltpu.VMEM((LEN, LEN), f32),
        pltpu.VMEM((LEN, LEN), f32),
        pltpu.VMEM((groups, LEN, STATE), f32),
        pltpu.VMEM((STATE, LEN), f32),
        pltpu.VMEM((groups, LEN, STATE), f32),
    ]


def mix_forward(proj, near, seg_col, seg_row, taps, taps_shared, heads):
    proj = pltpu.with_memory_space_constraint(proj, pltpu.HBM)
    rows, columns = proj.shape[0], proj.shape[1] - 3 * STATE
    groups = columns // WIDE
    return pl.pallas_call(
        mix_forward_kernel,
        grid=(rows // LEN, groups),
        in_specs=mixer_specs(columns),
        out_specs=[pl.BlockSpec((LEN, WIDE), lambda s, g: (s, g))] * 2,
        out_shape=[jax.ShapeDtypeStruct((rows, columns), f32), pltpu.HBM((rows, columns), f32)],
        scratch_shapes=mixer_scratch(groups),
        compiler_params=pltpu.CompilerParams(vmem_limit_bytes=VMEM),
        cost_estimate=pl.CostEstimate(flops=10**9, bytes_accessed=8 * 2**20, transcendentals=10**7),
        name="mix_forward",
    )(proj, proj, near, seg_col, seg_row, taps, taps_shared, heads)


def mix_backward(proj, near, seg_col, seg_row, taps, taps_shared, heads, ssd, dssd, mixed):
    rows, columns = proj.shape[0], proj.shape[1] - 3 * STATE
    groups, seqs = columns // WIDE, rows // LEN
    wide = pl.BlockSpec((LEN, WIDE), lambda s, g: (s, g))
    return pl.pallas_call(
        mix_backward_kernel,
        grid=(seqs, groups),
        in_specs=mixer_specs(columns) + [wide, wide, wide],
        out_specs=[
            pl.BlockSpec((LEN, columns + 3 * STATE), lambda s, g: (s, 0)),
            pl.BlockSpec((1, 8, columns + 3 * STATE), lambda s, g: (s, 0, 0)),
        ],
        out_shape=[
            pltpu.HBM(proj.shape, bf16),
            pltpu.HBM((seqs, 8, proj.shape[1]), f32),
        ],
        scratch_shapes=mixer_scratch(groups)
        + [
            pltpu.VMEM((LEN, STATE), bf16),
            pltpu.VMEM((LEN, STATE), bf16),
            pltpu.VMEM((LEN, LEN), f32),
            pltpu.VMEM((LEN, STATE), f32),
            pltpu.VMEM((LEN, STATE), f32),
        ],
        compiler_params=pltpu.CompilerParams(vmem_limit_bytes=WHOLE_VMEM),
        cost_estimate=pl.CostEstimate(flops=3 * 10**9, bytes_accessed=12 * 2**20, transcendentals=10**7),
        name="mix_backward",
    )(proj, proj, near, seg_col, seg_row, taps, taps_shared, heads, ssd, dssd, mixed)


SMALL = 8


def two_parts(rows):
    high = rows.astype(bf16).astype(f32)
    return [high, rows - high]


OVER_TOKENS = (((0,), (0,)), ((), ()))


def sum_small(ref, kept):
    tail = ref[kept : kept + 2 * SMALL].astype(f32)
    return tail[:SMALL] + tail[SMALL:]


def first_kernel(
    opposite_ref, near_ref, right_ref, small_ref, extra_ref, after_ref, before_ref
):
    times = lambda ref: lax.dot_general(
        ref[...], right_ref[...], OVER_TOKENS, preferred_element_type=f32
    )
    opposite, near = times(opposite_ref), times(near_ref)
    half = opposite.shape[0] // 2
    small = two_parts(small_ref[0] + small_ref[1] + extra_ref[...])
    for ref, rows in ((after_ref, slice(0, half)), (before_ref, slice(half, 2 * half))):
        ref[...] = jnp.concatenate([opposite[rows], near[rows]] + small, axis=0).astype(bf16)


def first_pieces(left, right, small, extra):
    rows, columns = left.shape[1] // SIDE, right.shape[1]
    wide = columns // 3
    return pl.pallas_call(
        first_kernel,
        grid=(3,),
        in_specs=[
            pl.BlockSpec((left.shape[0], rows), lambda j: (0, 1)),
            pl.BlockSpec((left.shape[0], rows), lambda j: (0, 2)),
            pl.BlockSpec((right.shape[0], wide), lambda j: (0, j)),
            pl.BlockSpec((2, SMALL, wide), lambda j: (0, 0, j)),
            pl.BlockSpec((SMALL, wide), lambda j: (0, j)),
        ],
        out_specs=[pl.BlockSpec((rows + 2 * SMALL, wide), lambda j: (0, j))] * 2,
        out_shape=[pltpu.HBM((rows + 2 * SMALL, columns), bf16)] * 2,
        compiler_params=pltpu.CompilerParams(vmem_limit_bytes=VMEM),
        cost_estimate=pl.CostEstimate(
            flops=4 * rows * columns * left.shape[0], bytes_accessed=6 * 2**20, transcendentals=0
        ),
        name="first_pieces",
    )(left, left, right, small, extra)


def second_kernel(own_left_ref, rest_left_ref, right_ref, own_ref, rest_ref):
    times = lambda ref: lax.dot_general(
        ref[...], right_ref[...], OVER_TOKENS, preferred_element_type=f32
    )
    own_ref[...] = times(own_left_ref)
    rest_ref[...] = times(rest_left_ref)


def second_pieces(left, right):
    rows, columns = left.shape[1] // SIDE, right.shape[1]
    wide = columns // 3
    block = lambda height: pl.BlockSpec((height, wide), lambda j: (0, j))
    return pl.pallas_call(
        second_kernel,
        grid=(3,),
        in_specs=[
            pl.BlockSpec((left.shape[0], rows), lambda j: (0, 0)),
            pl.BlockSpec((left.shape[0], rows), lambda j: (0, 3)),
            block(right.shape[0]),
        ],
        out_specs=[block(rows)] * 2,
        out_shape=[jax.ShapeDtypeStruct((rows, columns), f32)] * 2,
        compiler_params=pltpu.CompilerParams(vmem_limit_bytes=VMEM),
        cost_estimate=pl.CostEstimate(
            flops=4 * rows * columns * left.shape[0], bytes_accessed=9 * 2**20, transcendentals=0
        ),
        name="second_pieces",
    )(left, left, right)


def add_kernel(rest_ref, late_ref, behind_ref, ahead_ref, after_ref, before_ref):
    rows = rest_ref.shape[0]
    half = rows // 2
    late = late_ref[...]
    after = [rest_ref[:half] + behind_ref[:half].astype(f32)]
    after = after + two_parts(sum_small(behind_ref, rows) + late)
    after_ref[...] = jnp.concatenate(after, axis=0).astype(bf16)
    before = [rest_ref[half:] + ahead_ref[:half].astype(f32)] + two_parts(late)
    before_ref[...] = jnp.concatenate(before, axis=0).astype(bf16)


def added_pieces(rest, late, behind, ahead):
    rows, columns = rest.shape
    wide = columns // 5
    block = lambda height: pl.BlockSpec((height, wide), lambda j: (0, j))
    return pl.pallas_call(
        add_kernel,
        grid=(5,),
        in_specs=[block(rows), block(SMALL), block(behind.shape[0]), block(ahead.shape[0])],
        out_specs=[block(rows // 2 + 2 * SMALL)] * 2,
        out_shape=[pltpu.HBM((rows // 2 + 2 * SMALL, columns), bf16)] * 2,
        compiler_params=pltpu.CompilerParams(vmem_limit_bytes=VMEM),
        cost_estimate=pl.CostEstimate(flops=10**7, bytes_accessed=8 * 2**20, transcendentals=0),
        name="added_pieces",
    )(rest, late, behind, ahead)


def normed_kernel(
    core_ref, places_ref, dgate_ref, gate_ref, dproj_ref, normed_ref, gain_ref, *refs
):
    mix_refs = refs[:SIDE]
    own_ref, other_ref, row_ref, total = refs[SIDE:]
    step = pl.program_id(0)
    core = core_ref[0]
    turned = (((1,), (1,)), ((), ()))
    wide, width = gate_ref.shape[0], total.shape[1]
    spots = lax.broadcasted_iota(jnp.int32, (width, wide), 0)
    reorder = (spots == places_ref[...]).astype(f32).astype(bf16)
    for k, ref in enumerate(mix_refs):

        @pl.when(step == k)
        def _(k=k, ref=ref):
            back = lax.dot_general(dproj_ref[...], ref[...], turned, preferred_element_type=f32)
            back = lax.dot_general(
                back.astype(bf16), reorder, turned, preferred_element_type=f32
            )
            if k == 0:
                total[...] = back
            else:
                total[...] += back

    at = pl.ds(pl.multiple_of(step * wide, wide), wide)
    total[:, at] += lax.dot_general(dgate_ref[...], gate_ref[...], turned, preferred_element_type=f32)

    @pl.when(step == SIDE - 1)
    def _():
        own_ref[...] = total[pl.ds(pl.multiple_of(core * LEN, LEN), LEN), :]
        other = total[pl.ds(pl.multiple_of((1 - core) * LEN, LEN), LEN), :]
        other_ref[...] = other.astype(bf16)
        gain = jnp.sum(total[...] * normed_ref[...].astype(f32), axis=0, keepdims=True)
        gain = jnp.concatenate(
            [gain / gain_ref[...], jnp.zeros((1, row_ref.shape[1] - width), f32)], axis=1
        )
        row = lax.broadcasted_iota(jnp.int32, row_ref.shape, 0)
        row_ref[...] = jnp.where(row == SMALL - 1, gain, 0.0)


def normed_parts(core, places, dgate, w_rest, dproj, normed, gain, w_mix):
    rows, width = dgate.shape[0], places.shape[1]
    wide = width // SIDE
    full = lambda array: pl.BlockSpec(array.shape, lambda j: (0, 0))
    return pl.pallas_call(
        normed_kernel,
        grid=(SIDE,),
        in_specs=[
            pl.BlockSpec(memory_space=pltpu.SMEM),
            pl.BlockSpec((1, wide), lambda j: (0, j)),
            full(dgate),
            pl.BlockSpec((wide, dgate.shape[1]), lambda j: (j, 0)),
            full(dproj),
            full(normed),
            full(gain),
        ]
        + [full(piece) for piece in w_mix],
        out_specs=[pl.BlockSpec((LEN, width), lambda j: (0, 0))] * 2
        + [pl.BlockSpec((SMALL, dproj.shape[1]), lambda j: (0, 0))],
        out_shape=[
            jax.ShapeDtypeStruct((LEN, width), f32),
            jax.ShapeDtypeStruct((LEN, width), bf16),
            jax.ShapeDtypeStruct((SMALL, dproj.shape[1]), f32),
        ],
        scratch_shapes=[pltpu.VMEM((rows, width), f32)],
        compiler_params=pltpu.CompilerParams(vmem_limit_bytes=WHOLE_VMEM),
        cost_estimate=pl.CostEstimate(
            flops=10**10, bytes_accessed=24 * 2**20, transcendentals=0
        ),
        name="normed_parts",
    )(core, places, dgate, w_rest, dproj, normed, gain, *w_mix)


def branch_kernel(core_ref, own_mixed_ref, other_mixed_ref, out_ref, own_ref, other_ref, total):
    step = pl.program_id(0)
    core = core_ref[0]
    mixed = jnp.where(step // (SIDE // 2) == core, own_mixed_ref[...], other_mixed_ref[...])
    part = jnp.dot(mixed, out_ref[...], preferred_element_type=f32)

    @pl.when(step == 0)
    def _():
        total[...] = part

    @pl.when(step > 0)
    def _():
        total[...] += part

    @pl.when(step == SIDE - 1)
    def _():
        own_ref[...] = total[pl.ds(pl.multiple_of(core * LEN, LEN), LEN), :].astype(bf16)
        other = total[pl.ds(pl.multiple_of((1 - core) * LEN, LEN), LEN), :]
        other_ref[...] = other.astype(bf16)


def branch_parts(core, own_mixed, other_mixed, w_out):
    rows, half, width = own_mixed.shape[0], own_mixed.shape[1], w_out.shape[1]
    deep = 2 * half // SIDE
    mixed = pl.BlockSpec((rows, deep), lambda j: (0, j % (SIDE // 2)))
    return pl.pallas_call(
        branch_kernel,
        grid=(SIDE,),
        in_specs=[
            pl.BlockSpec(memory_space=pltpu.SMEM),
            mixed,
            mixed,
            pl.BlockSpec((deep, width), lambda j: (j, 0)),
        ],
        out_specs=[pl.BlockSpec((LEN, width), lambda j: (0, 0))] * 2,
        out_shape=[jax.ShapeDtypeStruct((LEN, width), bf16)] * 2,
        scratch_shapes=[pltpu.VMEM((rows, width), f32)],
        compiler_params=pltpu.CompilerParams(vmem_limit_bytes=WHOLE_VMEM),
        cost_estimate=pl.CostEstimate(
            flops=4 * rows * half * width, bytes_accessed=9 * 2**20, transcendentals=0
        ),
        name="branch_parts",
    )(core, own_mixed, other_mixed, w_out)


def store_parts(totals, small, out_refs):
    fill = out_refs[0].shape[0] - totals[0].shape[0] - 2 * SMALL
    fill = [jnp.zeros((fill, small.shape[1]), f32)] if fill else []
    for k, (total, out_ref) in enumerate(zip(totals, out_refs)):
        below = [small, jnp.zeros_like(small)] if k == 0 else two_parts(small)
        out_ref[...] = jnp.concatenate([total] + below + fill, axis=0).astype(out_ref.dtype)


def fold_first_kernel(
    own_ref, behind_ref, ahead_ref, behind_near_ref, ahead_near_ref, small_ref, extra_ref,
    late_ref, late_opposite_ref, *out_refs,
):
    kept = own_ref.shape[0]
    half, part = kept // 2, kept // SIDE
    small = small_ref[0] + small_ref[1] + extra_ref[...] + late_ref[...] + late_opposite_ref[...]
    small = small + sum_small(behind_ref, half) + sum_small(ahead_ref, half)
    small = small + sum_small(behind_near_ref, kept) + sum_small(ahead_near_ref, kept)
    totals = []
    for k in range(SIDE):
        at = k % (SIDE // 2) * part
        far, near = (behind_ref, ahead_near_ref) if k < SIDE // 2 else (ahead_ref, behind_near_ref)
        total = own_ref[k * part : (k + 1) * part] + far[at : at + part].astype(f32)
        totals.append(total + near[half + at : half + at + part].astype(f32))
    store_parts(totals, small, out_refs)


def fold_kernel(*refs):
    in_refs, out_refs = refs[:-SIDE], refs[-SIDE:]
    kept = (in_refs[0].shape[0] - 2 * SMALL) // 16 * 16
    part = kept // SIDE
    totals = [
        sum(ref[k * part : (k + 1) * part].astype(f32) for ref in in_refs) for k in range(SIDE)
    ]
    store_parts(totals, sum(sum_small(ref, kept) for ref in in_refs), out_refs)


def fold(kernel, arrays, kept):
    columns = arrays[0].shape[1]
    rows = -(-(kept // SIDE + 2 * SMALL) // 16) * 16
    steps = 5
    wide = columns // steps
    block = lambda height: pl.BlockSpec((height, wide), lambda j: (0, j))
    return pl.pallas_call(
        kernel,
        grid=(steps,),
        in_specs=[
            block(array.shape[0])
            if array.ndim == 2
            else pl.BlockSpec(array.shape[:2] + (wide,), lambda j: (0, 0, j))
            for array in arrays
        ],
        out_specs=[block(rows)] * SIDE,
        out_shape=[jax.ShapeDtypeStruct((rows, columns), f32)]
        + [pltpu.HBM((rows, columns), bf16)] * (SIDE - 1),
        compiler_params=pltpu.CompilerParams(vmem_limit_bytes=VMEM),
        cost_estimate=pl.CostEstimate(flops=10**7, bytes_accessed=8 * 2**20, transcendentals=0),
        name="fold",
    )(*arrays)


def columns_kernel(core_ref, in_ref, out_ref, mix_ref, rest_ref):
    first = core_ref[0] == 0
    rows, inner = in_ref.shape[0], out_ref.shape[1] * 2
    half, width = inner // 2, out_ref.shape[1] // 2
    pick = lambda one, two: jnp.where(first, one, two)
    rest_ref[:, :half] = pick(in_ref[:, :half], in_ref[:, half:inner])
    out = pick(out_ref[:, :width], out_ref[:, width:]).astype(f32)
    rest_ref[:, half : half + width] = out[:rows].astype(bf16)
    rest_ref[:, half + width :] = out[rows:].astype(bf16)
    mix_ref[:, :half] = pick(in_ref[:, inner : inner + half], in_ref[:, inner + half : 2 * inner])
    mix_ref[:, half : half + 2 * STATE] = in_ref[:, 2 * inner : 2 * inner + 2 * STATE]
    heads = (in_ref.shape[1] - 2 * inner - 2 * STATE) // 2
    dt = in_ref[:, 2 * inner + 2 * STATE :].astype(f32)
    dt = jnp.concatenate([dt, jnp.zeros((rows, STATE - 2 * heads), f32)], axis=1)
    dt = pick(dt, pltpu.roll(dt, STATE - heads, 1))
    lane = lax.broadcasted_iota(jnp.int32, dt.shape, 1)
    mix_ref[:, half + 2 * STATE :] = jnp.where(lane < heads, dt, 0.0).astype(bf16)


def core_columns(core, in_weight, out_weight):
    rows, width = in_weight.shape[0], out_weight.shape[1]
    whole = pl.BlockSpec(memory_space=pltpu.VMEM)
    return pl.pallas_call(
        columns_kernel,
        in_specs=[pl.BlockSpec(memory_space=pltpu.SMEM), whole, whole],
        out_specs=[whole, whole],
        out_shape=[
            jax.ShapeDtypeStruct((rows, width + 3 * STATE), bf16),
            jax.ShapeDtypeStruct((rows, 2 * width), bf16),
        ],
        name="core_columns",
    )(core, in_weight, out_weight)


def moved_kernel(core_ref, own_ref, other_ref, places_ref, leave_ref, normed_ref, moved_ref, left_ref):
    first = core_ref[0] == 0

    @pl.when(pl.program_id(0) == 0)
    def _():
        own, other = own_ref[...], other_ref[...]
        normed_ref[...] = jnp.concatenate(
            [jnp.where(first, own, other), jnp.where(first, other, own)], axis=0
        )

    normed = normed_ref[...]
    for order_ref, ref in ((places_ref, moved_ref), (leave_ref, left_ref)):
        order = order_ref[...]
        spots = lax.broadcasted_iota(jnp.int32, (normed.shape[1], order.shape[1]), 0)
        ones = (spots == order).astype(f32).astype(bf16)
        ref[...] = jnp.dot(normed, ones, preferred_element_type=f32).astype(bf16)


def moved_features(core, own, other, places, leave):
    rows, width = 2 * own.shape[0], own.shape[1]
    wide = width // SIDE
    full = pl.BlockSpec(own.shape, lambda j: (0, 0))
    row = pl.BlockSpec((1, wide), lambda j: (0, j))
    block = pl.BlockSpec((rows, wide), lambda j: (0, j))
    return pl.pallas_call(
        moved_kernel,
        grid=(SIDE,),
        in_specs=[pl.BlockSpec(memory_space=pltpu.SMEM), full, full, row, row],
        out_specs=[pl.BlockSpec((rows, width), lambda j: (0, 0)), block, block],
        out_shape=[jax.ShapeDtypeStruct((rows, width), bf16)] * 3,
        compiler_params=pltpu.CompilerParams(vmem_limit_bytes=VMEM),
        cost_estimate=pl.CostEstimate(
            flops=2 * 10**10, bytes_accessed=8 * 2**20, transcendentals=0
        ),
        name="moved_features",
    )(core, own, other, places[None], leave[None])


def finish_kernel(
    core_ref, own_ref, other_ref, rest_ref, rest_other_ref, in_ref, out_ref, taps_ref, bias_ref,
    dt_ref, log_ref, skip_ref, gain_ref, norm_ref,
):
    first = core_ref[0] == 0
    rows, half = in_ref.shape[0], gain_ref.shape[0] // 2
    width, rows_out = out_ref.shape[1] // 2, out_ref.shape[0]
    heads = dt_ref.shape[0] // 2

    def both(own, other):
        return jnp.concatenate([jnp.where(first, own, other), jnp.where(first, other, own)], axis=1)

    def two_heads(own, other):
        lane = lax.broadcasted_iota(jnp.int32, own.shape, 1)
        upper = pltpu.roll(jnp.where(first, other, own), heads, 1)
        return jnp.where(lane < heads, jnp.where(first, own, other), upper)

    rest, rest_other = rest_ref[...], rest_other_ref[...]
    out_ref[...] = both(rest[:rows_out], rest_other[:rows_out])
    gate = lambda got: jnp.concatenate(
        [got[rows_out : rows_out + rows], got[rows_out + rows :]], axis=1
    )
    in_ref[:, : 2 * half] = both(gate(rest), gate(rest_other))
    own, other = own_ref[...], other_ref[...]
    end = half + 2 * STATE
    at = 4 * half + 2 * STATE
    in_ref[:, 2 * half : 4 * half] = both(own[:rows, :half], other[:rows, :half])
    in_ref[:, 4 * half : at] = own[:rows, half:end] + other[:rows, half:end]
    in_ref[:, at:] = two_heads(own[:rows, end:], other[:rows, end:])[:, : 2 * heads]
    small = own[rows : rows + SMALL] + own[rows + SMALL : rows + 2 * SMALL]
    small_other = other[rows : rows + SMALL] + other[rows + SMALL : rows + 2 * SMALL]
    wide = both(small[:, :half], small_other[:, :half])
    shared = small[:, half:end] + small_other[:, half:end]
    taps_ref[:, : 2 * half] = wide[:TAPS]
    taps_ref[:, 2 * half :] = shared[:TAPS]
    bias_ref[...] = jnp.concatenate([wide[4:5], shared[4:5]], axis=1).reshape(bias_ref.shape)
    per_head = two_heads(small[:, end:], small_other[:, end:])
    dt_ref[...] = per_head[0, : 2 * heads]
    log_ref[...] = per_head[1, : 2 * heads]
    place = lax.broadcasted_iota(jnp.int32, (2 * half, STATE), 0) // HEAD
    ones = (place == lax.broadcasted_iota(jnp.int32, (2 * half, STATE), 1)).astype(f32)
    skip = jnp.dot(wide, ones, precision=highest, preferred_element_type=f32)
    skip_ref[...] = skip[5, : 2 * heads]
    gain_ref[...] = wide[6:7].reshape(gain_ref.shape)
    norm = small[7:8, : norm_ref.shape[0]] + small_other[7:8, : norm_ref.shape[0]]
    norm_ref[...] = norm.reshape(norm_ref.shape)


def finish(core, own, other, rest, rest_other, rows_in, rows_out, half, heads):
    width = 2 * rest.shape[1]
    shape = lambda *sizes: jax.ShapeDtypeStruct(sizes, f32)
    whole = pl.BlockSpec(memory_space=pltpu.VMEM)
    return pl.pallas_call(
        finish_kernel,
        in_specs=[pl.BlockSpec(memory_space=pltpu.SMEM)] + [whole] * 4,
        out_specs=[whole] * 9,
        out_shape=[
            shape(rows_in, 4 * half + 2 * STATE + 2 * heads),
            shape(rows_out, width),
            shape(TAPS, 2 * half + 2 * STATE),
            shape(2 * half + 2 * STATE),
            shape(2 * heads),
            shape(2 * heads),
            shape(2 * heads),
            shape(2 * half),
            shape(width),
        ],
        compiler_params=pltpu.CompilerParams(vmem_limit_bytes=VMEM),
        name="finish",
    )(core, own, other, rest, rest_other)


def owners_kernel(core_ref, own_ref, other_ref, cot_ref, normed_ref, dgate_ref, out_ref):
    shards, width = out_ref.shape[0], out_ref.shape[2]
    mine = pl.program_id(0) // (pl.num_programs(0) // 2) == core_ref[0]
    mixed = jnp.where(mine, own_ref[...], other_ref[...])
    grad_out = lax.dot_general(
        mixed, cot_ref[...], OVER_TOKENS, preferred_element_type=f32
    ).reshape(shards, -1, width)
    grad_gate = lax.dot_general(
        normed_ref[...], dgate_ref[...], OVER_TOKENS, preferred_element_type=f32
    )
    grad_gate = grad_gate.reshape(shards, -1, 2 * width)
    out_ref[...] = jnp.concatenate(
        [grad_out, grad_gate[:, :, :width], grad_gate[:, :, width:]], axis=1
    ).astype(bf16)


def owners_grads(core, own, other, cot, normed, dgate, shards):
    steps = 4
    each = shards // steps
    width = cot.shape[1]
    rows_out, rows_in = 2 * own.shape[1] // shards, normed.shape[1] // shards
    mixed = pl.BlockSpec((own.shape[0], each * rows_out), lambda j: (0, j % (steps // 2)))
    rows = rows_out + 2 * rows_in
    return pl.pallas_call(
        owners_kernel,
        grid=(steps,),
        in_specs=[
            pl.BlockSpec(memory_space=pltpu.SMEM),
            mixed,
            mixed,
            pl.BlockSpec(cot.shape, lambda j: (0, 0)),
            pl.BlockSpec((normed.shape[0], each * rows_in), lambda j: (0, j)),
            pl.BlockSpec(dgate.shape, lambda j: (0, 0)),
        ],
        out_specs=pl.BlockSpec((each, rows, width), lambda j: (j, 0, 0)),
        out_shape=pltpu.HBM((shards, rows, width), bf16),
        compiler_params=pltpu.CompilerParams(vmem_limit_bytes=VMEM),
        cost_estimate=pl.CostEstimate(
            flops=2 * cot.shape[0] * shards * rows * width, bytes_accessed=16 * 2**20, transcendentals=0
        ),
        name="owners_grads",
    )(core, own, other, cot, normed, dgate)


CHIPS = ("z", "y", "x")
ALL = ("grp",) + CHIPS
SIDE = 4
ORDERS = (("x", "y", "z"), ("y", "z", "x"))
GRAD_ORDERS = (("x", "y", "z"), ("x", "z", "y"))


def place(core, spot):
    index = core
    for axis in CHIPS:
        index = index * SIDE + spot[axis] % SIDE
    return index


def moved(value, phase, by, orders=GRAD_ORDERS):
    pairs = []
    for core in range(2):
        for z in range(SIDE):
            for y in range(SIDE):
                for x in range(SIDE):
                    spot = dict(z=z, y=y, x=x)
                    axis = orders[core][phase]
                    pairs.append((place(core, spot), place(core, {**spot, axis: spot[axis] + by})))
    return lax.ppermute(value, ALL, pairs)


def along(value, axis, by):
    return lax.ppermute(value, axis, [(i, (i + by) % SIDE) for i in range(SIDE)])


def swapped(value):
    return lax.ppermute(value, "grp", [(0, 1), (1, 0)])


def in_order(own, other, axis=0):
    first = lax.axis_index("grp") == 0
    return jnp.concatenate([jnp.where(first, own, other), jnp.where(first, other, own)], axis=axis)


def turned(value, dim, by):
    twice = jnp.concatenate([value, value], axis=dim)
    return lax.dynamic_slice_in_dim(twice, by, value.shape[dim], dim)


def gathered(own, orders, later):
    for phase in (2, 1):
        own = jnp.concatenate([own] + [moved(own, phase, -k, orders) for k in range(1, SIDE)])
    own, later = lax.optimization_barrier((own, later))
    after, before = moved(own, 0, -1, orders), moved(own, 0, 1, orders)
    middle = own.shape[0] // 2
    opposite = [moved(after[:middle], 0, -1, orders), moved(before[middle:], 0, 1, orders)]
    return [own, after, jnp.concatenate(opposite), before], later


def row_places(rows, orders):
    index = lax.iota(jnp.int32, SIDE**3 * rows)
    steps = (index // (SIDE * SIDE * rows), index // (SIDE * rows) % SIDE, index // rows % SIDE)
    core = lax.axis_index("grp")
    places = []
    for order in orders:
        spot = {axis: (lax.axis_index(axis) + step) % SIDE for axis, step in zip(order, steps)}
        places.append(((spot["z"] * SIDE + spot["y"]) * SIDE + spot["x"]) * rows + index % rows)
    return jnp.where(core == 0, places[0], places[1])


def halved(array, size, dim, other=False):
    core = lax.axis_index("grp")
    return lax.dynamic_slice_in_dim(array, (1 - core if other else core) * size, size, dim)


def times(left, right):
    return jnp.dot(left, right, preferred_element_type=f32)


def times_turned(left, right):
    return lax.dot_general(left, right, (((1,), (1,)), ((), ())), preferred_element_type=f32)


def on_device(
    tokens,
    segment_ids,
    norm_gain,
    in_weight,
    conv_weight,
    conv_bias,
    dt_bias,
    a_log,
    skip_d,
    gnorm_gain,
    out_weight,
    cotangent,
):
    width = tokens.shape[1]
    inner = gnorm_gain.shape[0]
    half = inner // 2
    heads = dt_bias.shape[0] // 2
    bc = conv_bias.shape[0] - inner
    rows_in, rows_out = in_weight.shape[0], out_weight.shape[0]
    shards = SIDE**3

    core = lax.axis_index("grp")
    which = core.astype(jnp.int32)[None]
    own_mix, own_rest = core_columns(which, in_weight, out_weight)
    w_rest = lax.all_gather(own_rest, CHIPS, axis=0, tiled=True)
    residual = tokens.astype(f32)
    scale = lax.rsqrt(jnp.mean(residual * residual, axis=-1, keepdims=True) + NORM_EPS)
    unit = residual * scale
    own_low = (unit * norm_gain).astype(bf16)
    places = row_places(rows_in, ORDERS)
    leave = row_places(rows_in, GRAD_ORDERS).reshape(2 * SIDE, -1)
    leave = jnp.concatenate([leave[k] for k in (0, 1, 4, 5, 3, 6, 2, 7)])
    w_mix, (normeds, orders) = gathered(
        own_mix, ORDERS, ((own_low, swapped(own_low)), (places, leave))
    )
    normed, normed_moved, left = moved_features(which, *normeds, *orders)
    places = orders[0]

    segments = in_order(segment_ids, swapped(segment_ids))
    near = [jnp.zeros(segments.shape, f32)]
    for back in range(1, TAPS):
        same = (segments[:, back:] == segments[:, :-back]).astype(f32)
        near.append(jnp.pad(same, ((0, 0), (back, 0))))
    near = jnp.stack(near + [near[0]] * 4, axis=-1).reshape(-1, 8)
    seg_col = segments.astype(f32).reshape(-1, 1)
    seg_row = segments.astype(f32)[:, None, :]
    cot_half = halved(in_order(cotangent, swapped(cotangent)), width // 2, 1)

    taps = jnp.concatenate(
        [
            halved(conv_weight[:, :inner], half, 1),
            halved(conv_bias[None, :inner], half, 1),
            jnp.repeat(halved(skip_d, heads, 0), HEAD)[None],
            halved(gnorm_gain[None], half, 1),
            jnp.zeros((1, half), f32),
        ]
    )
    taps_shared = jnp.concatenate(
        [conv_weight[:, inner:], conv_bias[None, inner:], jnp.zeros((3, bc), f32)]
    )
    head_rows = jnp.stack([halved(dt_bias, heads, 0), jnp.exp(halved(a_log, heads, 0))])
    head_rows = jnp.pad(head_rows, ((0, 6), (0, STATE - heads)))
    gain = halved(gnorm_gain, half, 0)

    quarter = width // SIDE
    proj = sum(
        times(normed_moved[:, k * quarter : (k + 1) * quarter], w_mix[k]) for k in range(SIDE)
    )
    sides = (near, seg_col, seg_row, taps, taps_shared, head_rows)
    ssd, mixed = mix_forward(proj, *sides)
    ssd, w_rest, cot_half, normed, left = lax.optimization_barrier(
        (ssd, w_rest, cot_half, normed, left)
    )
    w_out = jnp.stack(
        [
            w_rest[:, half : half + width // 2].reshape(shards, rows_in, -1),
            w_rest[:, half + width // 2 :].reshape(shards, rows_in, -1),
        ],
        axis=1,
    ).reshape(inner, -1)
    mixer_parts = times_turned(cot_half, w_out).astype(bf16)
    mixer_parts, normed = lax.optimization_barrier((mixer_parts, normed))
    gate_part = times(normed, w_rest[:, :half])
    grad_mixer = halved(mixer_parts, half, 1), swapped(halved(mixer_parts, half, 1, other=True))
    gate_part, grad_mixer = lax.optimization_barrier((gate_part, grad_mixer))
    grad_mixer = grad_mixer[0].astype(f32) + grad_mixer[1].astype(f32)
    opening = sigmoid(gate_part)
    gate = gate_part * opening
    gated = ssd * gate
    weighted = grad_mixer * gain
    sums = jnp.stack([jnp.sum(gated * gated, axis=-1), jnp.sum(gated * weighted, axis=-1)])
    sums = sums + swapped(sums)
    gscale = lax.rsqrt(sums[0] / inner + NORM_EPS)[:, None]
    pull = gscale * gscale * gscale * (sums[1] / inner)[:, None]
    mixer_low = (gated * gscale * gain).astype(bf16)
    mixer_low, ssd, gate_part, grad_mixer, gscale, pull = lax.optimization_barrier(
        (mixer_low, ssd, gate_part, grad_mixer, gscale, pull)
    )
    mixer_other = swapped(mixer_low)
    opening = sigmoid(gate_part)
    gate = gate_part * opening
    gated = ssd * gate
    dgated = gscale * (grad_mixer * gain) - gated * pull
    grad_gain = jnp.sum(grad_mixer * gated * gscale, axis=0)
    dgate_low = (dgated * ssd * silu_slope(gate_part, opening)).astype(bf16)
    dssd = (dgated * gate).astype(bf16)

    rest_grad = owners_grads(which, mixer_low, mixer_other, cot_half, normed, dgate_low, shards)
    rest_rows = rest_grad.shape[1]
    gain_row = jnp.zeros((SMALL, proj.shape[1]), f32).at[6, :half].set(grad_gain)
    rest_grad, dssd, gain_row = lax.optimization_barrier((rest_grad, dssd, gain_row))
    rest_share = lax.psum_scatter(
        rest_grad.reshape(shards * rest_rows, -1), ("z", "y"), scatter_dimension=0, tiled=True
    )

    dproj, drows = mix_backward(proj, *sides, ssd, dssd, mixed)
    leaving = (left, dproj, drows, gain_row)
    after, before = first_pieces(*leaving)

    dproj, after, before = lax.optimization_barrier((dproj, after, before))
    behind, ahead = moved(after, 0, 1), moved(before, 0, -1)
    normed_own, normed_other, late = normed_parts(
        which, places[None], dgate_low, w_rest, dproj, normed, norm_gain[None], w_mix
    )
    mixer_low, late = lax.optimization_barrier((mixer_low, late))
    branch_own, branch_other = branch_parts(which, mixer_low, mixer_other, w_out)
    dproj, branch_own = lax.optimization_barrier((dproj, branch_own))
    own, rest = second_pieces(left, dproj)
    behind, ahead, rest = lax.optimization_barrier((behind, ahead, rest))
    after, before = added_pieces(rest, late, behind, ahead)
    after, before, late, normed_other, branch_other = lax.optimization_barrier(
        (after, before, late, normed_other, branch_other)
    )
    sums = [own, moved(after, 0, 1), moved(before, 0, -1), behind, ahead, drows, gain_row, late]
    sums.append(moved(late, 0, 2))
    branch = in_order(branch_own, swapped(branch_other), axis=1)
    out_tokens = (residual + branch.astype(f32)).astype(bf16)
    grad_normed = normed_own + swapped(normed_other).astype(f32)
    q = grad_normed * norm_gain
    grad_tokens = cotangent.astype(f32) + scale * (
        q - unit * jnp.mean(q * unit, axis=-1, keepdims=True)
    )
    rest_turned = turned(rest_share.reshape(SIDE, rest_rows, -1), 0, lax.axis_index("x"))
    sums, rest_turned, out_tokens, grad_tokens = lax.optimization_barrier(
        (sums, rest_turned, out_tokens, grad_tokens)
    )
    own, *gone = fold(fold_first_kernel, sums, SIDE * SIDE * rows_in)

    gone, rest_turned = lax.optimization_barrier((gone, rest_turned))
    received = [own] + [moved(gone[k - 1], 1, k) for k in range(1, SIDE)]
    rest_total = rest_turned[0].astype(f32) + sum(
        along(rest_turned[k], "x", k).astype(f32) for k in range(1, SIDE)
    )
    received, rest_total = lax.optimization_barrier((received, rest_total))
    own, *gone = fold(fold_kernel, received, SIDE * rows_in)
    rest_other = swapped(rest_total)
    mix_total = own + sum(moved(gone[k - 1], 2, k).astype(f32) for k in range(1, SIDE))
    mix_other = swapped(mix_total)
    done = finish(
        which, mix_total, mix_other, rest_total, rest_other, rows_in, rows_out, half, heads
    )

    grad_in, grad_out, grad_taps, grad_bias, grad_dt, grad_log, grad_skip, grad_gated, grad_norm = done
    return (
        out_tokens,
        grad_tokens,
        grad_norm,
        grad_in,
        grad_taps,
        grad_bias,
        grad_dt,
        grad_log,
        grad_skip,
        grad_gated,
        grad_out,
    )


def solution(mesh):
    chips = Mesh(mesh.devices.reshape(2, SIDE, SIDE, SIDE), ALL)
    rows = P(ALL, None)
    owned = P(CHIPS, None)
    return jax.shard_map(
        on_device,
        mesh=chips,
        in_specs=(rows, rows, P(), owned, P(), P(), P(), P(), P(), P(), owned, rows),
        out_specs=(rows, rows, P(), owned, P(), P(), P(), P(), P(), P(), owned),
        check_vma=False,
    )
```
